512 devices in a mesh: lat: 32 (over z, core), wid: 16 (over x, y).
Axes of the slice: x: 4, y: 4, z: 16, core: 2. Of those that a mesh axis runs over, the one named last changes fastest.
Arguments:
- model_acts: bfloat16 [512, 4608], P(None, 'wid'), may hold values from -6 to 6
- picks: int32 [512, 64], replicated, may hold values from -1 to 32767, as said below
- group_ends: int32 [4], replicated, may hold values from 1 to 32768, as said below
- enc_weight: bfloat16 [4608, 32768], P('wid', 'lat'), may hold values from -0.09375 to 0.09375
- enc_bias: float32 [32768], P('lat'), may hold values from -3 to 3
- dec_weight: bfloat16 [32768, 4608], P('lat', 'wid'), may hold values from -1.5 to 1.5
- dec_bias: float32 [4608], P('wid'), may hold values from -3 to 3
Outputs:
- group_loss: float32 [512, 4], replicated
The draws below stay inside these ranges and needn't reach their ends.
Inputs may be any that keep to these rules, and one draw needn't show every extreme that they name: `picks`: the ids of one row are distinct; the filled slots of a row come first, then -1; every row has between 16 and 64 filled slots, and some row has all 64. `group_ends`: strictly increasing; the last equals 32768.
All inputs are finite; a program needn't handle non-finite values.
Results may differ from the reference program's by a relative error of at most 0.007.
Values may be sent and summed in bfloat16 or wider, within the bound.
A program may use at most 128 MiB of HBM per device.

```python
import math
import jax
import jax.numpy as jnp
from jax import lax

D = 4608
ROWS = 512
KMAX = 64
GROUPS = 4
LATENTS = 32768
N_WID = 16


def draw_picks(key, part):
    key = jax.random.fold_in(key, 11)
    key_noise, key_count = jax.random.split(key, 2)
    noise = jax.random.randint(key_noise, (ROWS, LATENTS), 0, 2 ** 14)
    scores = noise * LATENTS + jnp.arange(LATENTS, dtype=jnp.int32)[None, :]
    scores = scores.at[0, LATENTS - 1].set(2 ** 14 * LATENTS)
    top_scores, chosen = lax.top_k(scores, KMAX)
    counts = jax.random.randint(key_count, (ROWS,), KMAX // 4, KMAX + 1)
    counts = counts.at[0].set(KMAX).at[1].set(KMAX // 4)
    slots = jnp.arange(KMAX, dtype=jnp.int32)
    return jnp.where(slots[None, :] < counts[:, None], chosen, -1).astype(jnp.int32)


def draw_group_ends(key, part):
    key = jax.random.fold_in(key, 23)
    quarter = LATENTS // GROUPS
    offsets = jax.random.randint(key, (GROUPS,), 1, quarter + 1)
    ends = jnp.arange(GROUPS, dtype=jnp.int32) * quarter + offsets
    return ends.at[GROUPS - 1].set(LATENTS).astype(jnp.int32)


def steps_of(stream_key, extent, pieces, least, high):
    def one(dim, parts):
        draws = jax.random.uniform(jax.random.fold_in(jax.random.fold_in(stream_key, 6), dim), (parts,), jnp.float32, least / len(pieces), high / len(pieces))
        return jnp.repeat(jnp.exp(draws), extent[dim] // parts).reshape((-1,) + (1,) * (len(extent) - dim - 1))

    loudness = one(*pieces[0])
    for cut in pieces[1:]:
        loudness = loudness * one(*cut)
    return loudness


def normal_values(own_key, dims, scale, limit, cuts=(), kind=jnp.bfloat16):
    values = jax.random.normal(own_key, dims, jnp.float32) * scale
    if len(cuts) > 0:
        values = steps_of(own_key, dims, cuts, -0.22, 0.18) * values
    return jnp.clip(values, min=-limit, max=limit).astype(kind)


def setup_inputs(seed: int = 0) -> dict:
    seeds = jax.random.split(jax.random.key(seed), 8)
    return {
        "model_acts": normal_values(seeds[0], (ROWS, D), 1.0, 6.0, ((1, 16),)),
        "picks": draw_picks(jax.random.fold_in(seeds[7], 71), 0),
        "group_ends": draw_group_ends(jax.random.fold_in(seeds[7], 71), 0),
        "enc_weight": normal_values(seeds[3], (D, LATENTS), D ** -0.5, 0.09375, ((0, 16), (1, 32))),
        "enc_bias": normal_values(seeds[4], (LATENTS,), 0.5, 3.0, ((0, 32),), jnp.float32),
        "dec_weight": normal_values(seeds[5], (LATENTS, D), 16 ** -0.5, 1.5, ((0, 32), (1, 16))),
        "dec_bias": normal_values(seeds[6], (D,), 0.5, 3.0, ((0, 16),), jnp.float32),
    }


def reference(model_acts, picks, group_ends, enc_weight, enc_bias, dec_weight, dec_bias):
    shard_width = D // N_WID
    centered = model_acts.astype(jnp.float32) - dec_bias
    enc_in = centered.astype(jnp.bfloat16)
    enc_cols = jnp.transpose(enc_weight)
    block_rows = math.gcd(ROWS, 64)
    count_blocks = ROWS // block_rows

    def one_block(items):
        enc_part, cen_part, pick_part = items
        valid = pick_part >= 0
        safe_ids = jnp.maximum(pick_part, 0).astype(jnp.int32)
        columns = enc_cols[safe_ids].astype(jnp.float32)
        columns = columns.reshape(block_rows, KMAX, N_WID, shard_width)
        feature_parts = enc_part.astype(jnp.float32).reshape(block_rows, N_WID, shard_width)
        partial_sums = jnp.einsum("rwd,rkwd->rkw", feature_parts, columns)
        partial_sums = partial_sums.astype(jnp.bfloat16).astype(jnp.float32)
        preact = jnp.sum(partial_sums, axis=2) + enc_bias[safe_ids]
        acts = jnp.where(valid, jax.nn.relu(preact), 0.0).astype(jnp.bfloat16).astype(jnp.float32)
        dec_rows = dec_weight[safe_ids].astype(jnp.float32)
        losses = []
        for group in range(GROUPS):
            used = valid & (pick_part < group_ends[group])
            weights = jnp.where(used, acts, 0.0)
            prefix = jnp.einsum("rk,rkd->rd", weights, dec_rows)
            residual = cen_part - prefix
            losses.append(jnp.sum(residual * residual, axis=1) / D)
        return jnp.stack(losses, axis=1)

    result = lax.map(one_block, (enc_in.reshape(count_blocks, block_rows, D),
                                 centered.reshape(count_blocks, block_rows, D),
                                 picks.reshape(count_blocks, block_rows, KMAX)))
    return result.reshape(ROWS, GROUPS)
```

```python
import jax
import jax.numpy as jnp
from jax import lax
from jax.experimental import pallas as pl
from jax.experimental.pallas import tpu as pltpu
from jax.sharding import PartitionSpec as P

F32, BF16, I32 = jnp.float32, jnp.bfloat16, jnp.int32
ROWS, KMAX, GROUPS = 512, 64, 4
SHARD, MAIN = 288, 256
REM = SHARD - MAIN
LAT_DEV = 1024
N_LAT, N_WID, N_Z = 32, 16, 16
CHUNK = 16
WIDE = GROUPS * SHARD

LEVEL_1 = (
    (5, 1), (7, -1), (-7, 1), (-5, -1), (8, -2),
    (2, 1), (4, -1), (-4, 1), (-2, -1),
    (1, -1), (-1, 1),
)
CENTRES = (6, -6, 3, -3)
Z_PEERS = (1, -1, 2, -2, 3, -3, 6, -6)


def members(centre):
    return [k for k, (offset, dz) in enumerate(LEVEL_1) if offset + dz == centre]


def kernel(
    x_hbm, picks_hbm, ends_ref, encw_hbm, encb_hbm, dec_hbm, decb_hbm, out_ref,
    x_v, picks_v, encw_v, encb_v, dec_v, decb_v,
    xs, part, ids, lo_s, w0_s, w1_s, u0_t, u1_t, u0, u1, masked_dec,
    a1_src, a1_slot, acts_c, dens, to_sib, own, from_sib,
    l1_src, l1_slot, l2_src, l2_slot, c1_src, c1_slot, c2_src, c2_slot,
    in_sem, a1_send, a1_recv, a2_send, a2_recv, sib_send, sib_recv,
    l1_send, l1_recv, l2_send, l2_recv, c1_send, c1_recv, c2_send, c2_recv,
):
    lat = lax.axis_index("lat")
    wid = lax.axis_index("wid")
    z, core = lat // 2, lat % 2
    first = lat * LAT_DEV

    def in_plane(step):
        return (lat, lax.rem(wid + step, N_WID))

    def along_z(step):
        return (lax.rem(z + step + N_Z, N_Z) * 2 + core, wid)

    sibling = (lat + 1 - 2 * core, wid)

    def send(src, dst, s_sem, r_sem, device):
        return pltpu.make_async_remote_copy(
            src_ref=src, dst_ref=dst, send_sem=s_sem, recv_sem=r_sem,
            device_id=device, device_id_type=pl.DeviceIdType.MESH,
        )

    loads = [
        pltpu.make_async_copy(src, dst, in_sem.at[i])
        for i, (src, dst) in enumerate(
            ((x_hbm, x_v), (encw_hbm, encw_v), (decb_hbm, decb_v), (picks_hbm, picks_v),
             (encb_hbm, encb_v), (dec_hbm, dec_v))
        )
    ]
    for load in loads:
        load.start()

    barrier = pltpu.get_barrier_semaphore()

    def greet(device):
        pl.semaphore_signal(barrier, inc=1, device_id=device, device_id_type=pl.DeviceIdType.MESH)

    for step in Z_PEERS:
        greet(along_z(step))
    for step in range(1, N_WID):
        greet(in_plane(step))
    greet(sibling)

    loads[0].wait()
    loads[1].wait()
    loads[2].wait()
    x_t = x_v[...].astype(F32)
    tail = x_t[MAIN:, :]
    lanes_1 = lax.broadcasted_iota(I32, (1, 128), 1)
    bias_tail = jnp.concatenate([decb_v[:, MAIN:], jnp.zeros((1, 128 - REM), F32)], axis=1)
    bias_tail = jnp.where(lanes_1 < REM, bias_tail, 0.0)
    bias_tail = jnp.broadcast_to(bias_tail, (8, 128))
    bias_tail = (bias_tail + pltpu.roll(bias_tail, REM, 1)) + (
        pltpu.roll(bias_tail, 2 * REM, 1) + pltpu.roll(bias_tail, 3 * REM, 1))
    bias = jnp.concatenate([decb_v[:, :MAIN], bias_tail[:1, :]], axis=1)
    xs[...] = jnp.concatenate([x_t, tail, tail, tail], axis=0).T - bias
    part[...] = jnp.dot(
        xs[:, :SHARD].astype(BF16), encw_v[...], preferred_element_type=F32
    )

    loads[3].wait()
    loads[4].wait()
    local = picks_v[...] - first
    ids[...] = jnp.concatenate([local[:, :ROWS // 2], local[:, ROWS // 2:]], axis=0).T

    def picked(row):
        halves = []
        for sub in range(2):
            r = pl.multiple_of(row + 8 * sub, 8)
            r_2 = pl.multiple_of(row + 8 * sub + ROWS // 2, 8)
            where = ids[pl.ds(r, 8), :]
            lo, hi = where & 127, where >> 7
            lane = lax.broadcasted_iota(I32, (8, 128), 1)
            got = jnp.zeros((8, 128), F32)
            for h in range(8):
                cols = slice(128 * h, 128 * h + 128)
                here = jnp.where(
                    lane < KMAX,
                    jnp.take_along_axis(part[pl.ds(r, 8), cols], lo, 1, mode="promise_in_bounds"),
                    jnp.take_along_axis(part[pl.ds(r_2, 8), cols], lo, 1, mode="promise_in_bounds"),
                )
                got = jnp.where(hi == h, here, got)
            halves.append(got)
        return jnp.concatenate(halves, axis=0).astype(BF16)

    pl.semaphore_wait(barrier, len(Z_PEERS) + N_WID)

    def a1_copy(step):
        target = lax.rem(wid + step, N_WID)
        return send(a1_src.at[target], a1_slot.at[wid], a1_send.at[step], a1_recv.at[step], (lat, target))

    def a1_step(step, carry):
        target = lax.rem(wid + step, N_WID)
        a1_src[target] = picked(target * CHUNK)
        a1_copy(step).start()
        return carry

    lax.fori_loop(1, N_WID, a1_step, 0)
    my_rows = pl.multiple_of(wid * CHUNK, CHUNK)
    a1_slot[wid] = picked(my_rows)

    mine = ids[pl.ds(my_rows, CHUNK), :]
    hit = (mine >= 0) & (mine < LAT_DEV)
    my_bias = jnp.zeros((CHUNK, 128), F32)
    for h in range(8):
        row = jnp.broadcast_to(encb_v[:, 128 * h:128 * h + 128], (CHUNK, 128))
        my_bias = jnp.where(
            mine >> 7 == h, jnp.take_along_axis(row, mine & 127, 1, mode="promise_in_bounds"), my_bias)

    high = local >> 7
    inside = (local >= 0) & (local < LAT_DEV)
    field = (lax.broadcasted_iota(I32, local.shape, 0) + 1) << ((high & 3) * 8)
    lo_s[...] = local & 127
    w0_s[...] = jnp.where(inside & (high < 4), field, 0)
    w1_s[...] = jnp.where(inside & (high >= 4), field, 0)

    def fields(it, carry):
        cols = pl.ds(pl.multiple_of((it // 4) * 128, 128), 128)
        low = pl.multiple_of((it % 4) * 32, 32)
        iota = lax.broadcasted_iota(I32, (32, 128), 0) + low

        def eight(k8, acc):
            acc_0, acc_1 = acc
            rows = pl.ds(pl.multiple_of(k8 * 8, 8), 8)
            lo_8, w0_8, w1_8 = lo_s[rows, cols], w0_s[rows, cols], w1_s[rows, cols]
            for k in range(8):
                same = jnp.broadcast_to(lo_8[k:k + 1, :], (32, 128)) == iota
                acc_0 = acc_0 | jnp.where(same, jnp.broadcast_to(w0_8[k:k + 1, :], (32, 128)), 0)
                acc_1 = acc_1 | jnp.where(same, jnp.broadcast_to(w1_8[k:k + 1, :], (32, 128)), 0)
            return acc_0, acc_1

        zero = jnp.zeros((32, 128), I32)
        acc_0, acc_1 = lax.fori_loop(0, KMAX // 8, eight, (zero, zero))
        u0_t[pl.ds(low, 32), cols] = acc_0
        u1_t[pl.ds(low, 32), cols] = acc_1
        return carry

    lax.fori_loop(0, 16, fields, 0)
    u0[...] = u0_t[...].T
    u1[...] = u1_t[...].T

    for step in range(1, N_WID):
        a1_copy(step).wait_recv()
    total = jnp.zeros((CHUNK, 128), F32)
    for w in range(N_WID):
        total = total + a1_slot[w].astype(F32)
    acts_c[pl.ds(my_rows, CHUNK), :] = jnp.where(
        hit, jnp.maximum(total + my_bias, 0.0), 0.0).astype(BF16)

    def a2_copy(step):
        rows = acts_c.at[pl.ds(my_rows, CHUNK), :]
        return send(rows, rows, a2_send.at[step], a2_recv.at[step], in_plane(step))

    for step in range(1, N_WID):
        a2_copy(step).start()

    loads[5].wait()
    latent = lax.broadcasted_iota(I32, (1, LAT_DEV), 1) + first
    for g in range(GROUPS):
        keep = jnp.where(latent < ends_ref[g], 1.0, 0.0).astype(BF16)
        masked_dec[MAIN * g:MAIN * g + MAIN, :] = dec_v[:MAIN, :] * keep
        at = GROUPS * MAIN + REM * g
        masked_dec[at:at + REM, :] = dec_v[MAIN:, :] * keep

    for step in range(1, N_WID):
        a2_copy(step).wait_recv()

    lane_16 = lax.broadcasted_iota(I32, (16, 128), 1)

    def densify(half):
        def one(i, carry):
            r_c = pl.multiple_of(i * 16, 16)
            r = pl.multiple_of(half * (ROWS // 2) + i * 16, 16)
            values = pltpu.roll(acts_c[pl.ds(r_c, 16), :].astype(F32), 1 + KMAX * half, 1)
            values = jnp.where((lane_16 >= 1) & (lane_16 <= KMAX), values, 0.0)
            words = (u0[pl.ds(r, 16), :], u1[pl.ds(r, 16), :])
            for h in range(8):
                slot = (words[h // 4] >> (8 * (h % 4))) & 127
                dens[pl.ds(r, 16), 128 * h:128 * h + 128] = jnp.take_along_axis(
                    values, slot, 1, mode="promise_in_bounds").astype(BF16)
            return carry

        lax.fori_loop(0, ROWS // 32, one, 0)

    def decode(half):
        rows = pl.ds(pl.multiple_of(half * (ROWS // 2), ROWS // 2), ROWS // 2)
        return lax.dot_general(
            dens[rows, :], masked_dec[...], (((1,), (1,)), ((), ())), preferred_element_type=F32
        ).astype(BF16)

    def sib_copy(i):
        rows = pl.ds(64 * i, 64)
        return send(to_sib.at[rows], from_sib.at[rows], sib_send.at[i], sib_recv.at[i], sibling)

    densify(1 - core)
    to_sib[...] = decode(1 - core)
    for i in range(4):
        sib_copy(i).start()
    densify(core)
    own[...] = decode(core)
    for i in range(4):
        sib_copy(i).wait_recv()

    def chip_sum(offset):
        p = lax.rem(z - offset + N_Z, N_Z)
        rows = pl.ds(pl.multiple_of(p * CHUNK, CHUNK), CHUNK)
        return own[rows, :].astype(F32) + from_sib[rows, :].astype(F32)

    def l1_copy(k):
        return send(l1_src.at[k], l1_slot.at[k], l1_send.at[k], l1_recv.at[k], along_z(LEVEL_1[k][1]))

    def l2_copy(j):
        return send(l2_src.at[j], l2_slot.at[j], l2_send.at[j], l2_recv.at[j], along_z(-CENTRES[j]))

    for k, (offset, _) in enumerate(LEVEL_1):
        l1_src[k] = chip_sum(offset).astype(BF16)
        l1_copy(k).start()
    for j, centre in enumerate(CENTRES):
        acc = chip_sum(centre)
        for k in members(centre):
            l1_copy(k).wait_recv()
            acc = acc + l1_slot[k].astype(F32)
        l2_src[j] = acc.astype(BF16)
        l2_copy(j).start()
    prefix = chip_sum(0)
    for k in members(0):
        l1_copy(k).wait_recv()
        prefix = prefix + l1_slot[k].astype(F32)
    for j in (2, 3, 0, 1):
        l2_copy(j).wait_recv()
        prefix = prefix + l2_slot[j].astype(F32)

    row_0 = core * (ROWS // 2) + z * CHUNK
    centered = xs[pl.ds(pl.multiple_of(row_0, CHUNK), CHUNK), :]
    err_tail = centered[:, MAIN:] - prefix[:, GROUPS * MAIN:]
    sq_tail = err_tail * err_tail
    row_16 = lax.broadcasted_iota(I32, (16, 128), 0)
    placed = jnp.zeros((16, 128), F32)
    for g in range(GROUPS):
        err = centered[:, :MAIN] - prefix[:, MAIN * g:MAIN * g + MAIN]
        sq = err * err
        sq = sq[:, :128] + sq[:, 128:] + jnp.where(lane_16 // REM == g, sq_tail, 0.0)
        loss = jnp.sum(sq, axis=1, keepdims=True)
        placed = placed + jnp.where(lane_16 == lax.rem(z + g, 8) * 16 + row_16, loss, 0.0)
    partial = jnp.sum(placed, axis=0, keepdims=True)

    def c1_copy(step):
        return send(c1_src, c1_slot.at[wid], c1_send.at[step], c1_recv.at[step], in_plane(step))

    c1_src[...] = partial
    for step in range(1, N_WID):
        c1_copy(step).start()
    c1_slot[wid] = partial
    for step in range(1, N_WID):
        c1_copy(step).wait_recv()
    total_loss = c1_slot[0]
    for w in range(1, N_WID):
        total_loss = total_loss + c1_slot[w]
    total_loss = total_loss / (SHARD * N_WID)

    place = core * N_Z + z

    def c2_copy(step):
        return send(c2_src, c2_slot.at[place], c2_send.at[step], c2_recv.at[step],
                    (lax.rem(lat + step, N_LAT), wid))

    c2_src[...] = total_loss
    for step in range(1, N_LAT):
        c2_copy(step).start()
    c2_slot[place] = total_loss

    for step in range(1, N_WID):
        a1_copy(step).wait_send()
        a2_copy(step).wait_send()
        c1_copy(step).wait_send()
    for i in range(4):
        sib_copy(i).wait_send()
    for k in range(len(LEVEL_1)):
        l1_copy(k).wait_send()
    for j in range(len(CENTRES)):
        l2_copy(j).wait_send()
    for step in range(1, N_LAT):
        c2_copy(step).wait_recv()

    lane_8 = lax.broadcasted_iota(I32, (8, 128), 1)
    sub_8 = lax.broadcasted_iota(I32, (8, 128), 0)
    for b in range(ROWS // 128):
        block = jnp.concatenate([c2_slot[8 * b + m] for m in range(8)], axis=0)
        for g in range(GROUPS):
            line = jnp.sum(jnp.where(lane_8 // 16 == (sub_8 + g) % 8, block, 0.0), axis=0, keepdims=True)
            line = jnp.broadcast_to(line, (8, 128))
            if g:
                line = pltpu.roll(line, 128 - 16 * g, 1)
            out_ref[g:g + 1, 128 * b:128 * b + 128] = line[:1, :]
    for step in range(1, N_LAT):
        c2_copy(step).wait_send()


def body(model_acts, picks, group_ends, enc_weight, enc_bias, dec_weight, dec_bias):
    vmem, dma = pltpu.VMEM, pltpu.SemaphoreType.DMA
    half = ROWS // 2
    n_1, n_2 = len(LEVEL_1), len(CENTRES)
    anywhere = pl.BlockSpec(memory_space=pl.ANY)
    losses = pl.pallas_call(
        kernel,
        out_shape=jax.ShapeDtypeStruct((GROUPS, ROWS), F32),
        in_specs=[anywhere, anywhere, pl.BlockSpec(memory_space=pltpu.SMEM)] + [anywhere] * 4,
        out_specs=pl.BlockSpec(memory_space=pltpu.VMEM),
        scratch_shapes=[
            vmem((SHARD, ROWS), BF16), vmem((KMAX, ROWS), I32), vmem((SHARD, LAT_DEV), BF16),
            vmem((1, LAT_DEV), F32), vmem((SHARD, LAT_DEV), BF16), vmem((1, SHARD), F32),
            vmem((ROWS, MAIN + 128), F32), vmem((ROWS, LAT_DEV), F32), vmem((half, 128), I32),
            vmem((KMAX, ROWS), I32), vmem((KMAX, ROWS), I32), vmem((KMAX, ROWS), I32),
            vmem((128, ROWS), I32), vmem((128, ROWS), I32), vmem((ROWS, 128), I32), vmem((ROWS, 128), I32),
            vmem((WIDE, LAT_DEV), BF16),
            vmem((N_WID, CHUNK, 128), BF16), vmem((N_WID, CHUNK, 128), BF16), vmem((half, 128), BF16),
            vmem((ROWS, LAT_DEV), BF16), vmem((half, WIDE), BF16), vmem((half, WIDE), BF16),
            vmem((half, WIDE), BF16),
            vmem((n_1, CHUNK, WIDE), BF16), vmem((n_1, CHUNK, WIDE), BF16),
            vmem((n_2, CHUNK, WIDE), BF16), vmem((n_2, CHUNK, WIDE), BF16),
            vmem((1, 128), F32), vmem((N_WID, 1, 128), F32), vmem((1, 128), F32), vmem((N_LAT, 1, 128), F32),
            dma((6,)), dma((N_WID,)), dma((N_WID,)), dma((N_WID,)), dma((N_WID,)), dma((4,)), dma((4,)),
            dma((n_1,)), dma((n_1,)), dma((n_2,)), dma((n_2,)),
            dma((N_WID,)), dma((N_WID,)), dma((N_LAT,)), dma((N_LAT,)),
        ],
        compiler_params=pltpu.CompilerParams(
            collective_id=0, has_side_effects=True, vmem_limit_bytes=48 * 2 ** 20),
    )(
        model_acts.T, picks.T, group_ends, enc_weight, enc_bias.reshape(1, -1), dec_weight.T,
        dec_bias.reshape(1, -1),
    )
    return losses.T


def solution(mesh):
    placed = (P(None, "wid"), P(), P(), P("wid", "lat"), P("lat"), P("lat", "wid"), P("wid"))
    return jax.shard_map(body, mesh=mesh, in_specs=placed, out_specs=P(), check_vma=False)
```

```python
import jax
import jax.numpy as jnp
from jax import lax
from jax.experimental import pallas as pl
from jax.experimental.pallas import tpu as pltpu
from jax.sharding import PartitionSpec as P

F32, BF16, I32 = jnp.float32, jnp.bfloat16, jnp.int32
ROWS, KMAX, GROUPS = 512, 64, 4
SHARD, MAIN = 288, 256
REM = SHARD - MAIN
LAT_DEV = 1024
EXTRACT = 32
N_LAT, N_WID, N_Z = 32, 16, 16
CHUNK = 16
WIDE = GROUPS * SHARD

LEVEL_1 = (
    (5, 1), (7, -1), (-7, 1), (-5, -1), (8, -2),
    (2, 1), (4, -1), (-4, 1), (-2, -1),
    (1, -1), (-1, 1),
)
CENTRES = (6, -6, 3, -3)
Z_PEERS = (3, -3, 2, -2, 1, -1)


def ring(step, size):
    return min(step % size, -step % size)


PLANE = sorted(
    ((dx, dy) for dx in range(4) for dy in range(4) if dx or dy),
    key=lambda d: -(ring(d[0], 4) + ring(d[1], 4)))
COLUMN = sorted(
    ((dz, dc) for dz in range(N_Z) for dc in range(2) if dz or dc), key=lambda d: -ring(d[0], N_Z))
ARRIVALS = (range(14, 4, -1), range(4, -1, -1))


def members(centre):
    return [k for k, (offset, dz) in enumerate(LEVEL_1) if offset + dz == centre]


def kernel(
    x_hbm, picks_hbm, ends_ref, encw_hbm, encb_hbm, dec_hbm, decb_v, out_ref,
    x_v, picks_v, encw_v, encb_v, dec_v,
    xs, part, ids, lo_s, w0_s, w1_s, u0_t, u1_t, u0, u1, masked_dec,
    a1_src, a1_slot, acts_c, dens, to_sib, own, from_sib,
    l1_src, l1_slot, l2_src, l2_slot, c1_src, c1_slot, c2_src, c2_slot,
    in_sem, a1_send, a1_recv, a2_send, a2_recv, sib_send, sib_recv,
    far_ready, l1_send, l1_recv, l2_send, l2_recv, c1_send, c1_recv, c2_send, c2_recv,
):
    lat = lax.axis_index("lat")
    wid = lax.axis_index("wid")
    z, core = lat // 2, lat % 2
    first = lat * LAT_DEV

    def plane(j, sign=1):
        dx, dy = PLANE[j]
        return (wid // 4 + 4 + sign * dx) % 4 * 4 + (wid % 4 + 4 + sign * dy) % 4

    def in_plane(j):
        return (lat, plane(j))

    def along_z(step):
        return (lax.rem(z + step + N_Z, N_Z) * 2 + core, wid)

    sibling = (lat + 1 - 2 * core, wid)

    def send(src, dst, s_sem, r_sem, device):
        return pltpu.make_async_remote_copy(
            src_ref=src, dst_ref=dst, send_sem=s_sem, recv_sem=r_sem,
            device_id=device, device_id_type=pl.DeviceIdType.MESH,
        )

    loads = [
        pltpu.make_async_copy(src, dst, in_sem.at[i])
        for i, (src, dst) in enumerate(
            ((x_hbm, x_v), (encw_hbm, encw_v), (picks_hbm, picks_v),
             (encb_hbm, encb_v), (dec_hbm, dec_v))
        )
    ]
    barrier = pltpu.get_barrier_semaphore()

    def greet(device):
        pl.semaphore_signal(barrier, inc=1, device_id=device, device_id_type=pl.DeviceIdType.MESH)

    for step in Z_PEERS:
        greet(along_z(step))
    for j in range(len(PLANE)):
        greet(in_plane(j))
    greet(sibling)
    for load in loads:
        load.start()
    pending = []

    loads[0].wait()
    loads[1].wait()
    x_t = x_v[...].astype(F32)
    tail = x_t[MAIN:, :]
    lanes_1 = lax.broadcasted_iota(I32, (1, 128), 1)
    bias_tail = jnp.concatenate([decb_v[MAIN:].reshape(1, REM), jnp.zeros((1, 128 - REM), F32)], axis=1)
    bias_tail = jnp.where(lanes_1 < REM, bias_tail, 0.0)
    bias_tail = jnp.broadcast_to(bias_tail, (8, 128))
    bias_tail = (bias_tail + pltpu.roll(bias_tail, REM, 1)) + (
        pltpu.roll(bias_tail, 2 * REM, 1) + pltpu.roll(bias_tail, 3 * REM, 1))
    bias = jnp.concatenate([decb_v[:MAIN].reshape(1, MAIN), bias_tail[:1, :]], axis=1)
    xs[...] = jnp.concatenate([x_t, tail, tail, tail], axis=0).T - bias
    part[...] = jnp.dot(
        xs[:, :SHARD].astype(BF16), encw_v[...], preferred_element_type=F32
    )

    loads[2].wait()
    loads[3].wait()
    local = picks_v[...] - first
    ids[...] = jnp.concatenate([local[:, :ROWS // 2], local[:, ROWS // 2:]], axis=0).T

    lane_e = lax.broadcasted_iota(I32, (EXTRACT, 128), 1)

    def extract(i, carry):
        r = pl.multiple_of(i * EXTRACT, EXTRACT)
        r_2 = pl.multiple_of(i * EXTRACT + ROWS // 2, EXTRACT)
        where = ids[pl.ds(r, EXTRACT), :]
        lo, hi = where & 127, where >> 7
        got = jnp.zeros((EXTRACT, 128), F32)
        for h in range(8):
            cols = slice(128 * h, 128 * h + 128)
            here = jnp.where(
                lane_e < KMAX,
                jnp.take_along_axis(part[pl.ds(r, EXTRACT), cols], lo, 1, mode="promise_in_bounds"),
                jnp.take_along_axis(part[pl.ds(r_2, EXTRACT), cols], lo, 1, mode="promise_in_bounds"),
            )
            got = jnp.where(hi == h, here, got)
        a1_src[pl.ds(r, EXTRACT), :] = got.astype(BF16)
        return carry

    lax.fori_loop(0, ROWS // 2 // EXTRACT, extract, 0)

    pl.semaphore_wait(barrier, len(Z_PEERS) + N_WID)
    def a1_copy(j):
        target = plane(j)
        rows = pl.ds(pl.multiple_of(target * CHUNK, CHUNK), CHUNK)
        return send(a1_src.at[rows], a1_slot.at[wid], a1_send.at[j], a1_recv.at[j], (lat, target))

    for j in range(len(PLANE)):
        a1_copy(j).start()
        pending.append(a1_copy(j))
    for i, step in enumerate((3, -3)):
        pl.semaphore_signal(
            far_ready.at[i], inc=1, device_id=along_z(step), device_id_type=pl.DeviceIdType.MESH)
    my_rows = pl.multiple_of(wid * CHUNK, CHUNK)
    a1_slot[wid] = a1_src[pl.ds(my_rows, CHUNK), :]

    mine = ids[pl.ds(my_rows, CHUNK), :]
    hit = (mine >= 0) & (mine < LAT_DEV)
    my_bias = jnp.zeros((CHUNK, 128), F32)
    for h in range(8):
        row = jnp.broadcast_to(encb_v[:, 128 * h:128 * h + 128], (CHUNK, 128))
        my_bias = jnp.where(
            mine >> 7 == h, jnp.take_along_axis(row, mine & 127, 1, mode="promise_in_bounds"), my_bias)

    high = local >> 7
    inside = (local >= 0) & (local < LAT_DEV)
    field = (lax.broadcasted_iota(I32, local.shape, 0) + 1) << ((high & 3) * 8)
    lo_s[...] = local & 127
    w0_s[...] = jnp.where(inside & (high < 4), field, 0)
    w1_s[...] = jnp.where(inside & (high >= 4), field, 0)

    def fields(it, carry):
        cols = pl.ds(pl.multiple_of((it // 4) * 128, 128), 128)
        low = pl.multiple_of((it % 4) * 32, 32)
        iota = lax.broadcasted_iota(I32, (32, 128), 0) + low

        def eight(k8, acc):
            acc_0, acc_1 = acc
            rows = pl.ds(pl.multiple_of(k8 * 8, 8), 8)
            lo_8, w0_8, w1_8 = lo_s[rows, cols], w0_s[rows, cols], w1_s[rows, cols]
            for k in range(8):
                same = jnp.broadcast_to(lo_8[k:k + 1, :], (32, 128)) == iota
                acc_0 = acc_0 | jnp.where(same, jnp.broadcast_to(w0_8[k:k + 1, :], (32, 128)), 0)
                acc_1 = acc_1 | jnp.where(same, jnp.broadcast_to(w1_8[k:k + 1, :], (32, 128)), 0)
            return acc_0, acc_1

        zero = jnp.zeros((32, 128), I32)
        acc_0, acc_1 = lax.fori_loop(0, KMAX // 8, eight, (zero, zero))
        u0_t[pl.ds(low, 32), cols] = acc_0
        u1_t[pl.ds(low, 32), cols] = acc_1
        return carry

    lax.fori_loop(0, 16, fields, 0)
    u0[...] = u0_t[...].T
    u1[...] = u1_t[...].T

    loads[4].wait()
    latent = lax.broadcasted_iota(I32, (1, LAT_DEV), 1) + first
    for g in range(GROUPS):
        keep = jnp.where(latent < ends_ref[g], 1.0, 0.0).astype(BF16)
        masked_dec[MAIN * g:MAIN * g + MAIN, :] = dec_v[:MAIN, :] * keep
        at = GROUPS * MAIN + REM * g
        masked_dec[at:at + REM, :] = dec_v[MAIN:, :] * keep

    for j in range(len(PLANE)):
        a1_copy(j).wait_recv()
    total = jnp.zeros((CHUNK, 128), F32)
    for w in range(N_WID):
        total = total + a1_slot[w].astype(F32)
    acts_c[pl.ds(my_rows, CHUNK), :] = jnp.where(
        hit, jnp.maximum(total + my_bias, 0.0), 0.0).astype(BF16)

    def a2_copy(j):
        rows = acts_c.at[pl.ds(my_rows, CHUNK), :]
        return send(rows, rows, a2_send.at[j], a2_recv.at[j], in_plane(j))

    for j in range(len(PLANE)):
        a2_copy(j).start()
        pending.append(a2_copy(j))

    lane_16 = lax.broadcasted_iota(I32, (16, 128), 1)

    def densify(w):
        packed = acts_c[pl.ds(pl.multiple_of(w * CHUNK, CHUNK), CHUNK), :].astype(F32)
        for half in range(2):
            values = pltpu.roll(packed, 1 + KMAX * half, 1)
            values = jnp.where((lane_16 >= 1) & (lane_16 <= KMAX), values, 0.0)
            rows = pl.ds(pl.multiple_of(half * (ROWS // 2) + w * CHUNK, CHUNK), CHUNK)
            words = (u0[rows, :], u1[rows, :])
            for h in range(8):
                slot = (words[h // 4] >> (8 * (h % 4))) & 127
                dens[rows, 128 * h:128 * h + 128] = jnp.take_along_axis(
                    values, slot, 1, mode="promise_in_bounds").astype(BF16)

    densify(wid)
    for group in ARRIVALS:
        for j in group:
            a2_copy(j).wait_recv()
        for j in group:
            densify(plane(j, -1))

    def decode(half, cols):
        rows = pl.ds(pl.multiple_of(half * (ROWS // 2), ROWS // 2), ROWS // 2)
        return lax.dot_general(
            dens[rows, :], masked_dec[cols, :], (((1,), (1,)), ((), ())), preferred_element_type=F32
        ).astype(BF16)

    pieces = [slice(MAIN * g, min(MAIN * g + MAIN, WIDE)) for g in range(GROUPS + 1)]

    def sib_copy(i):
        return send(to_sib.at[:, pieces[i]], from_sib.at[:, pieces[i]], sib_send.at[i], sib_recv.at[i], sibling)

    for i, cols in enumerate(pieces):
        to_sib[:, cols] = decode(1 - core, cols)
        sib_copy(i).start()
        pending.append(sib_copy(i))
    for cols in pieces:
        own[:, cols] = decode(core, cols)
    for i in range(len(pieces)):
        sib_copy(i).wait_recv()

    def chip_sum(offset):
        p = lax.rem(z - offset + N_Z, N_Z)
        rows = pl.ds(pl.multiple_of(p * CHUNK, CHUNK), CHUNK)
        return own[rows, :].astype(F32) + from_sib[rows, :].astype(F32)

    def l1_copy(k):
        return send(l1_src.at[k], l1_slot.at[k], l1_send.at[k], l1_recv.at[k], along_z(LEVEL_1[k][1]))

    def l2_copy(j):
        return send(l2_src.at[j], l2_slot.at[j], l2_send.at[j], l2_recv.at[j], along_z(-CENTRES[j]))

    for k, (offset, _) in enumerate(LEVEL_1):
        l1_src[k] = chip_sum(offset).astype(BF16)
        l1_copy(k).start()
        pending.append(l1_copy(k))
    for i in range(2):
        pl.semaphore_wait(far_ready.at[i], 1)
    for j, centre in enumerate(CENTRES):
        acc = chip_sum(centre)
        for k in members(centre):
            l1_copy(k).wait_recv()
            acc = acc + l1_slot[k].astype(F32)
        l2_src[j] = acc.astype(BF16)
        l2_copy(j).start()
        pending.append(l2_copy(j))
    prefix = chip_sum(0)
    for k in members(0):
        l1_copy(k).wait_recv()
        prefix = prefix + l1_slot[k].astype(F32)
    for j in (2, 3, 0, 1):
        l2_copy(j).wait_recv()
        prefix = prefix + l2_slot[j].astype(F32)

    row_0 = core * (ROWS // 2) + z * CHUNK
    centered = xs[pl.ds(pl.multiple_of(row_0, CHUNK), CHUNK), :]
    err_tail = centered[:, MAIN:] - prefix[:, GROUPS * MAIN:]
    sq_tail = err_tail * err_tail
    row_16 = lax.broadcasted_iota(I32, (16, 128), 0)
    placed = jnp.zeros((16, 128), F32)
    for g in range(GROUPS):
        err = centered[:, :MAIN] - prefix[:, MAIN * g:MAIN * g + MAIN]
        sq = err * err
        sq = sq[:, :128] + sq[:, 128:] + jnp.where(lane_16 // REM == g, sq_tail, 0.0)
        loss = jnp.sum(sq, axis=1, keepdims=True)
        placed = placed + jnp.where(lane_16 == lax.rem(z + g, 8) * 16 + row_16, loss, 0.0)
    partial = jnp.sum(placed, axis=0, keepdims=True)

    def c1_copy(j):
        return send(c1_src, c1_slot.at[wid], c1_send.at[j], c1_recv.at[j], in_plane(j))

    c1_src[...] = partial
    for j in range(len(PLANE)):
        c1_copy(j).start()
        pending.append(c1_copy(j))
    c1_slot[wid] = partial
    for j in range(len(PLANE)):
        c1_copy(j).wait_recv()
    total_loss = c1_slot[0]
    for w in range(1, N_WID):
        total_loss = total_loss + c1_slot[w]
    total_loss = total_loss / (SHARD * N_WID)

    place = core * N_Z + z

    def c2_copy(j):
        dz, dc = COLUMN[j]
        target = (z + dz) % N_Z * 2 + (core + dc) % 2
        return send(c2_src, c2_slot.at[place], c2_send.at[j], c2_recv.at[j], (target, wid))

    c2_src[...] = total_loss
    for j in range(len(COLUMN)):
        c2_copy(j).start()
        pending.append(c2_copy(j))
    c2_slot[place] = total_loss
    for copy in pending:
        copy.wait_send()
    for j in range(len(COLUMN)):
        c2_copy(j).wait_recv()

    lane_8 = lax.broadcasted_iota(I32, (8, 128), 1)
    sub_8 = lax.broadcasted_iota(I32, (8, 128), 0)
    for b in range(ROWS // 128):
        block = jnp.concatenate([c2_slot[8 * b + m] for m in range(8)], axis=0)
        for g in range(GROUPS):
            line = jnp.sum(jnp.where(lane_8 // 16 == (sub_8 + g) % 8, block, 0.0), axis=0, keepdims=True)
            line = jnp.broadcast_to(line, (8, 128))
            if g:
                line = pltpu.roll(line, 128 - 16 * g, 1)
            out_ref[g:g + 1, 128 * b:128 * b + 128] = line[:1, :]


def body(model_acts, picks, group_ends, enc_weight, enc_bias, dec_weight, dec_bias):
    vmem, dma = pltpu.VMEM, pltpu.SemaphoreType.DMA
    half = ROWS // 2
    n_1, n_2 = len(LEVEL_1), len(CENTRES)
    anywhere = pl.BlockSpec(memory_space=pl.ANY)
    losses = pl.pallas_call(
        kernel,
        out_shape=jax.ShapeDtypeStruct((GROUPS, ROWS), F32),
        in_specs=[anywhere, anywhere, pl.BlockSpec(memory_space=pltpu.SMEM)] + [anywhere] * 3
        + [pl.BlockSpec(memory_space=pltpu.VMEM)],
        out_specs=pl.BlockSpec(memory_space=pltpu.VMEM),
        scratch_shapes=[
            vmem((SHARD, ROWS), BF16), vmem((KMAX, ROWS), I32), vmem((SHARD, LAT_DEV), BF16),
            vmem((1, LAT_DEV), F32), vmem((SHARD, LAT_DEV), BF16),
            vmem((ROWS, MAIN + 128), F32), vmem((ROWS, LAT_DEV), F32), vmem((half, 128), I32),
            vmem((KMAX, ROWS), I32), vmem((KMAX, ROWS), I32), vmem((KMAX, ROWS), I32),
            vmem((128, ROWS), I32), vmem((128, ROWS), I32), vmem((ROWS, 128), I32), vmem((ROWS, 128), I32),
            vmem((WIDE, LAT_DEV), BF16),
            vmem((half, 128), BF16), vmem((N_WID, CHUNK, 128), BF16), vmem((half, 128), BF16),
            vmem((ROWS, LAT_DEV), BF16), vmem((half, WIDE), BF16), vmem((half, WIDE), BF16),
            vmem((half, WIDE), BF16),
            vmem((n_1, CHUNK, WIDE), BF16), vmem((n_1, CHUNK, WIDE), BF16),
            vmem((n_2, CHUNK, WIDE), BF16), vmem((n_2, CHUNK, WIDE), BF16),
            vmem((1, 128), F32), vmem((N_WID, 1, 128), F32), vmem((1, 128), F32), vmem((N_LAT, 1, 128), F32),
            dma((5,)), dma((N_WID,)), dma((N_WID,)), dma((N_WID,)), dma((N_WID,)), dma((GROUPS + 1,)), dma((GROUPS + 1,)),
            pltpu.SemaphoreType.REGULAR((2,)), dma((n_1,)), dma((n_1,)), dma((n_2,)), dma((n_2,)),
            dma((N_WID,)), dma((N_WID,)), dma((N_LAT,)), dma((N_LAT,)),
        ],
        compiler_params=pltpu.CompilerParams(
            collective_id=0, has_side_effects=True, vmem_limit_bytes=56 * 2 ** 20),
    )(
        model_acts.T, picks.T, group_ends, enc_weight, enc_bias.reshape(1, -1), dec_weight.T,
        dec_bias,
    )
    return losses.T


def solution(mesh):
    placed = (P(None, "wid"), P(), P(), P("wid", "lat"), P("lat"), P("lat", "wid"), P("wid"))
    return jax.shard_map(body, mesh=mesh, in_specs=placed, out_specs=P(), check_vma=False)
```

```python
import jax
import jax.numpy as jnp
from jax import lax
from jax.experimental import pallas as pl
from jax.experimental.pallas import tpu as pltpu
from jax.sharding import PartitionSpec as P

F32, BF16, I32 = jnp.float32, jnp.bfloat16, jnp.int32
ROWS, KMAX, GROUPS = 512, 64, 4
SHARD, MAIN = 288, 256
REM = SHARD - MAIN
LAT_DEV = 1024
EXTRACT = 64
N_LAT, N_WID, N_Z = 32, 16, 16
CHUNK = 16
WIDE = GROUPS * SHARD

LEVEL_1 = (
    (5, 1), (7, -1), (-7, 1), (-5, -1), (8, -2),
    (2, 1), (4, -1), (-4, 1), (-2, -1),
    (1, -1), (-1, 1),
)
LEVEL_1 = (LEVEL_1, LEVEL_1[:4] + ((-8, 2),) + LEVEL_1[5:])
CENTRES = (6, -6, 3, -3)
PIECES = (slice(0, 768), slice(768, WIDE))
Z_PEERS = (3, -3, 2, -2, 1, -1)


def ring(step, size):
    return min(step % size, -step % size)


PLANE = sorted(
    ((dx, dy) for dx in range(4) for dy in range(4) if dx or dy),
    key=lambda d: -(ring(d[0], 4) + ring(d[1], 4)))
COLUMN = sorted(
    ((dz, dc) for dz in range(N_Z) for dc in range(2) if dz or dc), key=lambda d: -ring(d[0], N_Z))
ARRIVALS = (range(14, 10, -1), range(10, 4, -1), range(4, -1, -1))


def members(i, centre):
    return [k for k, (offset, dz) in enumerate(LEVEL_1[i % 2]) if offset + dz == centre]


def kernel(
    x_hbm, picks_hbm, ends_ref, encw_hbm, encb_hbm, dec_hbm, decb_v, out_ref,
    x_v, picks_v, encw_v, encb_v, dec_v,
    xs, part, ids, lo_s, w0_s, w1_s, u0_t, u1_t, u0, u1, masked_dec,
    a1_src, a1_slot, acts_c, dens, to_sib, own, from_sib,
    l1_src, l1_slot, l2_src, l2_slot, c1_src, c1_slot, c2_src, c2_slot,
    in_sem, a1_send, a1_recv, a2_send, a2_recv, sib_send, sib_recv,
    l1_send, l1_recv, l2_send, l2_recv, c1_send, c1_recv, c2_send, c2_recv,
):
    lat = lax.axis_index("lat")
    wid = lax.axis_index("wid")
    z, core = lat // 2, lat % 2
    first = lat * LAT_DEV

    def plane(j, sign=1):
        dx, dy = PLANE[j]
        return (wid // 4 + 4 + sign * dx) % 4 * 4 + (wid % 4 + 4 + sign * dy) % 4

    def in_plane(j):
        return (lat, plane(j))

    def along_z(step):
        return (lax.rem(z + step + N_Z, N_Z) * 2 + core, wid)

    sibling = (lat + 1 - 2 * core, wid)

    def send(src, dst, s_sem, r_sem, device):
        return pltpu.make_async_remote_copy(
            src_ref=src, dst_ref=dst, send_sem=s_sem, recv_sem=r_sem,
            device_id=device, device_id_type=pl.DeviceIdType.MESH,
        )

    loads = [
        pltpu.make_async_copy(src, dst, in_sem.at[i])
        for i, (src, dst) in enumerate(
            ((x_hbm, x_v), (encw_hbm, encw_v), (picks_hbm, picks_v),
             (encb_hbm, encb_v), (dec_hbm, dec_v))
        )
    ]
    for load in loads:
        load.start()
    barrier = pltpu.get_barrier_semaphore()

    def greet(device):
        pl.semaphore_signal(barrier, inc=1, device_id=device, device_id_type=pl.DeviceIdType.MESH)

    for step in Z_PEERS:
        greet(along_z(step))
    for j in range(len(PLANE)):
        greet(in_plane(j))
    greet(sibling)
    pending = []

    for load in loads[:4]:
        load.wait()
    x_t = x_v[...].astype(F32)
    tail = x_t[MAIN:, :]
    lanes_1 = lax.broadcasted_iota(I32, (1, 128), 1)
    bias_tail = jnp.concatenate([decb_v[MAIN:].reshape(1, REM), jnp.zeros((1, 128 - REM), F32)], axis=1)
    bias_tail = jnp.where(lanes_1 < REM, bias_tail, 0.0)
    bias_tail = jnp.broadcast_to(bias_tail, (8, 128))
    bias_tail = (bias_tail + pltpu.roll(bias_tail, REM, 1)) + (
        pltpu.roll(bias_tail, 2 * REM, 1) + pltpu.roll(bias_tail, 3 * REM, 1))
    bias = jnp.concatenate([decb_v[:MAIN].reshape(1, MAIN), bias_tail[:1, :]], axis=1)
    xs[...] = jnp.concatenate([x_t, tail, tail, tail], axis=0).T - bias
    part[...] = jnp.dot(
        xs[:, :SHARD].astype(BF16), encw_v[...], preferred_element_type=F32
    )

    local = picks_v[...] - first
    ids[...] = jnp.concatenate([local[:, :ROWS // 2], local[:, ROWS // 2:]], axis=0).T

    lane_e = lax.broadcasted_iota(I32, (EXTRACT, 128), 1)

    def extract(i, carry):
        r = pl.multiple_of(i * EXTRACT, EXTRACT)
        r_2 = pl.multiple_of(i * EXTRACT + ROWS // 2, EXTRACT)
        where = ids[pl.ds(r, EXTRACT), :]
        lo, hi = where & 127, where >> 7
        got = jnp.zeros((EXTRACT, 128), F32)
        for h in range(8):
            cols = slice(128 * h, 128 * h + 128)
            here = jnp.where(
                lane_e < KMAX,
                jnp.take_along_axis(part[pl.ds(r, EXTRACT), cols], lo, 1, mode="promise_in_bounds"),
                jnp.take_along_axis(part[pl.ds(r_2, EXTRACT), cols], lo, 1, mode="promise_in_bounds"),
            )
            got = jnp.where(hi == h, here, got)
        a1_src[pl.ds(r, EXTRACT), :] = got.astype(BF16)
        return carry

    lax.fori_loop(0, ROWS // 2 // EXTRACT, extract, 0)

    pl.semaphore_wait(barrier, len(Z_PEERS) + N_WID)
    def a1_copy(j):
        target = plane(j)
        rows = pl.ds(pl.multiple_of(target * CHUNK, CHUNK), CHUNK)
        return send(a1_src.at[rows], a1_slot.at[wid], a1_send.at[j], a1_recv.at[j], (lat, target))

    for j in range(len(PLANE)):
        a1_copy(j).start()
        pending.append(a1_copy(j))
    my_rows = pl.multiple_of(wid * CHUNK, CHUNK)
    a1_slot[wid] = a1_src[pl.ds(my_rows, CHUNK), :]

    mine = ids[pl.ds(my_rows, CHUNK), :]
    hit = (mine >= 0) & (mine < LAT_DEV)
    my_bias = jnp.zeros((CHUNK, 128), F32)
    for h in range(8):
        row = jnp.broadcast_to(encb_v[:, 128 * h:128 * h + 128], (CHUNK, 128))
        my_bias = jnp.where(
            mine >> 7 == h, jnp.take_along_axis(row, mine & 127, 1, mode="promise_in_bounds"), my_bias)

    high = local >> 7
    inside = (local >= 0) & (local < LAT_DEV)
    field = (lax.broadcasted_iota(I32, local.shape, 0) + 1) << ((high & 3) * 8)
    lo_s[...] = local & 127
    w0_s[...] = jnp.where(inside & (high < 4), field, 0)
    w1_s[...] = jnp.where(inside & (high >= 4), field, 0)

    def fields(it, carry):
        cols = pl.ds(pl.multiple_of((it // 4) * 128, 128), 128)
        low = pl.multiple_of((it % 4) * 32, 32)
        iota = lax.broadcasted_iota(I32, (32, 128), 0) + low

        def eight(k8, acc):
            acc_0, acc_1 = acc
            rows = pl.ds(pl.multiple_of(k8 * 8, 8), 8)
            lo_8, w0_8, w1_8 = lo_s[rows, cols], w0_s[rows, cols], w1_s[rows, cols]
            for k in range(8):
                same = jnp.broadcast_to(lo_8[k:k + 1, :], (32, 128)) == iota
                acc_0 = acc_0 | jnp.where(same, jnp.broadcast_to(w0_8[k:k + 1, :], (32, 128)), 0)
                acc_1 = acc_1 | jnp.where(same, jnp.broadcast_to(w1_8[k:k + 1, :], (32, 128)), 0)
            return acc_0, acc_1

        zero = jnp.zeros((32, 128), I32)
        acc_0, acc_1 = lax.fori_loop(0, KMAX // 8, eight, (zero, zero))
        u0_t[pl.ds(low, 32), cols] = acc_0
        u1_t[pl.ds(low, 32), cols] = acc_1
        return carry

    lax.fori_loop(0, 16, fields, 0)
    u0[...] = u0_t[...].T
    u1[...] = u1_t[...].T

    loads[4].wait()
    latent = lax.broadcasted_iota(I32, (1, LAT_DEV), 1) + first
    for g in range(GROUPS):
        keep = jnp.where(latent < ends_ref[g], 1.0, 0.0).astype(BF16)
        masked_dec[MAIN * g:MAIN * g + MAIN, :] = dec_v[:MAIN, :] * keep
        at = GROUPS * MAIN + REM * g
        masked_dec[at:at + REM, :] = dec_v[MAIN:, :] * keep

    for j in range(len(PLANE)):
        a1_copy(j).wait_recv()
    total = jnp.zeros((CHUNK, 128), F32)
    for w in range(N_WID):
        total = total + a1_slot[w].astype(F32)
    acts_c[pl.ds(my_rows, CHUNK), :] = jnp.where(
        hit, jnp.maximum(total + my_bias, 0.0), 0.0).astype(BF16)

    def a2_copy(j):
        rows = acts_c.at[pl.ds(my_rows, CHUNK), :]
        return send(rows, rows, a2_send.at[j], a2_recv.at[j], in_plane(j))

    for j in range(len(PLANE)):
        a2_copy(j).start()
        pending.append(a2_copy(j))

    lane_16 = lax.broadcasted_iota(I32, (16, 128), 1)

    def densify(w):
        packed = acts_c[pl.ds(pl.multiple_of(w * CHUNK, CHUNK), CHUNK), :].astype(F32)
        for half in range(2):
            values = pltpu.roll(packed, 1 + KMAX * half, 1)
            values = jnp.where((lane_16 >= 1) & (lane_16 <= KMAX), values, 0.0)
            rows = pl.ds(pl.multiple_of(half * (ROWS // 2) + w * CHUNK, CHUNK), CHUNK)
            words = (u0[rows, :], u1[rows, :])
            for h in range(8):
                slot = (words[h // 4] >> (8 * (h % 4))) & 127
                dens[rows, 128 * h:128 * h + 128] = jnp.take_along_axis(
                    values, slot, 1, mode="promise_in_bounds").astype(BF16)

    densify(wid)
    for group in ARRIVALS:
        for j in group:
            a2_copy(j).wait_recv()
        for j in group:
            densify(plane(j, -1))

    def decode(half, cols):
        rows = pl.ds(pl.multiple_of(half * (ROWS // 2), ROWS // 2), ROWS // 2)
        return lax.dot_general(
            dens[rows, :], masked_dec[cols, :], (((1,), (1,)), ((), ())), preferred_element_type=F32
        ).astype(BF16)

    def sib_copy(i):
        cols = PIECES[i]
        return send(to_sib.at[:, cols], from_sib.at[:, cols], sib_send.at[i], sib_recv.at[i], sibling)

    def chip_sum(i, offset):
        p = lax.rem(z - offset + N_Z, N_Z)
        rows = pl.ds(pl.multiple_of(p * CHUNK, CHUNK), CHUNK)
        return own[rows, PIECES[i]].astype(F32) + from_sib[rows, PIECES[i]].astype(F32)

    def l1_copy(i, k):
        return send(l1_src.at[k, :, PIECES[i]], l1_slot.at[k, :, PIECES[i]], l1_send.at[i, k], l1_recv.at[i, k],
                    along_z(LEVEL_1[i % 2][k][1]))

    def l2_copy(i, j):
        step = -3 if CENTRES[j] > 0 else 3
        return send(l2_src.at[j, :, PIECES[i]], l2_slot.at[j, :, PIECES[i]], l2_send.at[i, j], l2_recv.at[i, j],
                    along_z(step))

    def l1_sum(i, centre):
        acc = chip_sum(i, centre)
        for k in members(i, centre):
            l1_copy(i, k).wait_recv()
            acc = acc + l1_slot[k, :, PIECES[i]].astype(F32)
        return acc

    for i, cols in enumerate(PIECES):
        to_sib[:, cols] = decode(1 - core, cols)
        sib_copy(i).start()
        pending.append(sib_copy(i))
    for i, cols in enumerate(PIECES):
        own[:, cols] = decode(core, cols)
        sib_copy(i).wait_recv()
        for k, (offset, _) in enumerate(LEVEL_1[i % 2]):
            l1_src[k, :, cols] = chip_sum(i, offset).astype(BF16)
            l1_copy(i, k).start()
            pending.append(l1_copy(i, k))

    for i, cols in enumerate(PIECES):
        for j in (0, 1):
            l2_src[j, :, cols] = l1_sum(i, CENTRES[j]).astype(BF16)
            l2_copy(i, j).start()
            pending.append(l2_copy(i, j))
    for i, cols in enumerate(PIECES):
        for j in (2, 3):
            acc = l1_sum(i, CENTRES[j])
            l2_copy(i, j - 2).wait_recv()
            l2_src[j, :, cols] = (acc + l2_slot[j - 2, :, cols].astype(F32)).astype(BF16)
            l2_copy(i, j).start()
            pending.append(l2_copy(i, j))
    parts = []
    for i, cols in enumerate(PIECES):
        acc = l1_sum(i, 0)
        for j in (2, 3):
            l2_copy(i, j).wait_recv()
            acc = acc + l2_slot[j, :, cols].astype(F32)
        parts.append(acc)
    prefix = jnp.concatenate(parts, axis=1)
    row_0 = core * (ROWS // 2) + z * CHUNK
    centered = xs[pl.ds(pl.multiple_of(row_0, CHUNK), CHUNK), :]
    err_tail = centered[:, MAIN:] - prefix[:, GROUPS * MAIN:]
    sq_tail = err_tail * err_tail
    row_16 = lax.broadcasted_iota(I32, (16, 128), 0)
    placed = jnp.zeros((16, 128), F32)
    for g in range(GROUPS):
        err = centered[:, :MAIN] - prefix[:, MAIN * g:MAIN * g + MAIN]
        sq = err * err
        sq = sq[:, :128] + sq[:, 128:] + jnp.where(lane_16 // REM == g, sq_tail, 0.0)
        loss = jnp.sum(sq, axis=1, keepdims=True)
        placed = placed + jnp.where(lane_16 == lax.rem(z + g, 8) * 16 + row_16, loss, 0.0)
    partial = jnp.sum(placed, axis=0, keepdims=True)

    def c1_copy(j):
        return send(c1_src, c1_slot.at[wid], c1_send.at[j], c1_recv.at[j], in_plane(j))

    c1_src[...] = partial
    for j in range(len(PLANE)):
        c1_copy(j).start()
        pending.append(c1_copy(j))
    c1_slot[wid] = partial
    for j in range(len(PLANE)):
        c1_copy(j).wait_recv()
    total_loss = c1_slot[0]
    for w in range(1, N_WID):
        total_loss = total_loss + c1_slot[w]
    total_loss = total_loss / (SHARD * N_WID)

    place = core * N_Z + z

    def c2_copy(j):
        dz, dc = COLUMN[j]
        target = (z + dz) % N_Z * 2 + (core + dc) % 2
        return send(c2_src, c2_slot.at[place], c2_send.at[j], c2_recv.at[j], (target, wid))

    c2_src[...] = total_loss
    for j in range(len(COLUMN)):
        c2_copy(j).start()
        pending.append(c2_copy(j))
    c2_slot[place] = total_loss
    for copy in pending:
        copy.wait_send()
    for j in range(len(COLUMN)):
        c2_copy(j).wait_recv()

    lane_8 = lax.broadcasted_iota(I32, (8, 128), 1)
    sub_8 = lax.broadcasted_iota(I32, (8, 128), 0)
    for b in range(ROWS // 128):
        block = jnp.concatenate([c2_slot[8 * b + m] for m in range(8)], axis=0)
        for g in range(GROUPS):
            line = jnp.sum(jnp.where(lane_8 // 16 == (sub_8 + g) % 8, block, 0.0), axis=0, keepdims=True)
            line = jnp.broadcast_to(line, (8, 128))
            if g:
                line = pltpu.roll(line, 128 - 16 * g, 1)
            out_ref[g:g + 1, 128 * b:128 * b + 128] = line[:1, :]


def body(model_acts, picks, group_ends, enc_weight, enc_bias, dec_weight, dec_bias):
    vmem, dma = pltpu.VMEM, pltpu.SemaphoreType.DMA
    half = ROWS // 2
    n_1, n_2, n_p = len(LEVEL_1[0]), len(CENTRES), len(PIECES)
    anywhere = pl.BlockSpec(memory_space=pl.ANY)
    losses = pl.pallas_call(
        kernel,
        out_shape=jax.ShapeDtypeStruct((GROUPS, ROWS), F32),
        in_specs=[anywhere, anywhere, pl.BlockSpec(memory_space=pltpu.SMEM)] + [anywhere] * 3
        + [pl.BlockSpec(memory_space=pltpu.VMEM)],
        out_specs=pl.BlockSpec(memory_space=pltpu.VMEM),
        scratch_shapes=[
            vmem((SHARD, ROWS), BF16), vmem((KMAX, ROWS), I32), vmem((SHARD, LAT_DEV), BF16),
            vmem((1, LAT_DEV), F32), vmem((SHARD, LAT_DEV), BF16),
            vmem((ROWS, MAIN + 128), F32), vmem((ROWS, LAT_DEV), F32), vmem((half, 128), I32),
            vmem((KMAX, ROWS), I32), vmem((KMAX, ROWS), I32), vmem((KMAX, ROWS), I32),
            vmem((128, ROWS), I32), vmem((128, ROWS), I32), vmem((ROWS, 128), I32), vmem((ROWS, 128), I32),
            vmem((WIDE, LAT_DEV), BF16),
            vmem((half, 128), BF16), vmem((N_WID, CHUNK, 128), BF16), vmem((half, 128), BF16),
            vmem((ROWS, LAT_DEV), BF16), vmem((half, WIDE), BF16), vmem((half, WIDE), BF16),
            vmem((half, WIDE), BF16),
            vmem((n_1, CHUNK, WIDE), BF16), vmem((n_1, CHUNK, WIDE), BF16),
            vmem((n_2, CHUNK, WIDE), BF16), vmem((n_2, CHUNK, WIDE), BF16),
            vmem((1, 128), F32), vmem((N_WID, 1, 128), F32), vmem((1, 128), F32), vmem((N_LAT, 1, 128), F32),
            dma((5,)), dma((N_WID,)), dma((N_WID,)), dma((N_WID,)), dma((N_WID,)), dma((n_p,)), dma((n_p,)),
            dma((n_p, n_1)), dma((n_p, n_1)), dma((n_p, n_2)), dma((n_p, n_2)),
            dma((N_WID,)), dma((N_WID,)), dma((N_LAT,)), dma((N_LAT,)),
        ],
        compiler_params=pltpu.CompilerParams(
            collective_id=0, has_side_effects=True, vmem_limit_bytes=56 * 2 ** 20),
    )(
        model_acts.T, picks.T, group_ends, enc_weight, enc_bias.reshape(1, -1), dec_weight.T,
        dec_bias,
    )
    return losses.T


def solution(mesh):
    placed = (P(None, "wid"), P(), P(), P("wid", "lat"), P("lat"), P("lat", "wid"), P("wid"))
    return jax.shard_map(body, mesh=mesh, in_specs=placed, out_specs=P(), check_vma=False)
```

```python
import jax
import jax.numpy as jnp
from jax import lax
from jax.experimental import pallas as pl
from jax.experimental.pallas import tpu as pltpu
from jax.sharding import PartitionSpec as P

F32, BF16, I32 = jnp.float32, jnp.bfloat16, jnp.int32
ROWS, KMAX, GROUPS = 512, 64, 4
SHARD, MAIN = 288, 256
REM = SHARD - MAIN
LAT_DEV = 1024
EXTRACT = 64
N_LAT, N_WID, N_Z = 32, 16, 16
CHUNK = 16
WIDE = GROUPS * SHARD

LEVEL_1 = (
    (5, 1), (7, -1), (-7, 1), (-5, -1), (8, -2),
    (2, 1), (4, -1), (-4, 1), (-2, -1),
    (1, -1), (-1, 1),
)
LEVEL_1 = (LEVEL_1, LEVEL_1[:4] + ((-8, 2),) + LEVEL_1[5:])
CENTRES = (6, -6, 3, -3)
PIECES = (slice(0, 384), slice(384, WIDE))
Z_PEERS = (3, -3, 2, -2, 1, -1)


def ring(step, size):
    return min(step % size, -step % size)


PLANE = sorted(
    ((dx, dy) for dx in range(4) for dy in range(4) if dx or dy),
    key=lambda d: -(ring(d[0], 4) + ring(d[1], 4)))
COLUMN = sorted(
    ((dz, dc) for dz in range(N_Z) for dc in range(2) if dz or dc), key=lambda d: -ring(d[0], N_Z))
ARRIVALS = (range(14, 10, -1), range(10, 4, -1), range(4, -1, -1))


def members(i, centre):
    return [k for k, (offset, dz) in enumerate(LEVEL_1[i % 2]) if offset + dz == centre]


def kernel(
    x_hbm, picks_hbm, ends_ref, encw_hbm, encb_hbm, dec_hbm, decb_v, out_ref,
    x_v, picks_v, encw_v, encb_v, dec_v,
    xs, part, ids, lo_s, w0_s, w1_s, u0_t, u1_t, u0, u1, masked_dec,
    a1_src, a1_slot, acts_c, dens, to_sib, own, from_sib,
    l1_src, l1_slot, l2_src, l2_slot, c1_src, c1_slot, c2_src, c2_slot,
    in_sem, a1_send, a1_recv, a2_send, a2_recv, sib_send, sib_recv,
    l1_send, l1_recv, l2_send, l2_recv, c1_send, c1_recv, c2_send, c2_recv,
):
    lat = lax.axis_index("lat")
    wid = lax.axis_index("wid")
    z, core = lat // 2, lat % 2
    first = lat * LAT_DEV

    def plane(j, sign=1):
        dx, dy = PLANE[j]
        return (wid // 4 + 4 + sign * dx) % 4 * 4 + (wid % 4 + 4 + sign * dy) % 4

    def in_plane(j):
        return (lat, plane(j))

    def along_z(step):
        return (lax.rem(z + step + N_Z, N_Z) * 2 + core, wid)

    sibling = (lat + 1 - 2 * core, wid)

    def send(src, dst, s_sem, r_sem, device):
        return pltpu.make_async_remote_copy(
            src_ref=src, dst_ref=dst, send_sem=s_sem, recv_sem=r_sem,
            device_id=device, device_id_type=pl.DeviceIdType.MESH,
        )

    loads = [
        pltpu.make_async_copy(src, dst, in_sem.at[i])
        for i, (src, dst) in enumerate(
            ((x_hbm, x_v), (encw_hbm, encw_v), (picks_hbm, picks_v),
             (encb_hbm, encb_v), (dec_hbm, dec_v))
        )
    ]
    for load in loads:
        load.start()
    barrier = pltpu.get_barrier_semaphore()

    def greet(device):
        pl.semaphore_signal(barrier, inc=1, device_id=device, device_id_type=pl.DeviceIdType.MESH)

    for step in Z_PEERS:
        greet(along_z(step))
    for j in range(len(PLANE)):
        greet(in_plane(j))
    greet(sibling)
    pending = []

    for load in loads[:4]:
        load.wait()
    x_t = x_v[...].astype(F32)
    tail = x_t[MAIN:, :]
    lanes_1 = lax.broadcasted_iota(I32, (1, 128), 1)
    bias_tail = jnp.concatenate([decb_v[MAIN:].reshape(1, REM), jnp.zeros((1, 128 - REM), F32)], axis=1)
    bias_tail = jnp.where(lanes_1 < REM, bias_tail, 0.0)
    bias_tail = jnp.broadcast_to(bias_tail, (8, 128))
    bias_tail = (bias_tail + pltpu.roll(bias_tail, REM, 1)) + (
        pltpu.roll(bias_tail, 2 * REM, 1) + pltpu.roll(bias_tail, 3 * REM, 1))
    bias = jnp.concatenate([decb_v[:MAIN].reshape(1, MAIN), bias_tail[:1, :]], axis=1)
    xs[...] = jnp.concatenate([x_t, tail, tail, tail], axis=0).T - bias
    part[...] = jnp.dot(
        xs[:, :SHARD].astype(BF16), encw_v[...], preferred_element_type=F32
    )

    local = picks_v[...] - first
    ids[...] = jnp.concatenate([local[:, :ROWS // 2], local[:, ROWS // 2:]], axis=0).T

    lane_e = lax.broadcasted_iota(I32, (EXTRACT, 128), 1)

    def extract(i, carry):
        r = pl.multiple_of(i * EXTRACT, EXTRACT)
        r_2 = pl.multiple_of(i * EXTRACT + ROWS // 2, EXTRACT)
        where = ids[pl.ds(r, EXTRACT), :]
        lo, hi = where & 127, where >> 7
        got = jnp.zeros((EXTRACT, 128), F32)
        for h in range(8):
            cols = slice(128 * h, 128 * h + 128)
            here = jnp.where(
                lane_e < KMAX,
                jnp.take_along_axis(part[pl.ds(r, EXTRACT), cols], lo, 1, mode="promise_in_bounds"),
                jnp.take_along_axis(part[pl.ds(r_2, EXTRACT), cols], lo, 1, mode="promise_in_bounds"),
            )
            got = jnp.where(hi == h, here, got)
        a1_src[pl.ds(r, EXTRACT), :] = got.astype(BF16)
        return carry

    lax.fori_loop(0, ROWS // 2 // EXTRACT, extract, 0)

    pl.semaphore_wait(barrier, len(Z_PEERS) + N_WID)
    def a1_copy(j):
        target = plane(j)
        rows = pl.ds(pl.multiple_of(target * CHUNK, CHUNK), CHUNK)
        return send(a1_src.at[rows], a1_slot.at[wid], a1_send.at[j], a1_recv.at[j], (lat, target))

    for j in range(len(PLANE)):
        a1_copy(j).start()
        pending.append(a1_copy(j))
    my_rows = pl.multiple_of(wid * CHUNK, CHUNK)
    a1_slot[wid] = a1_src[pl.ds(my_rows, CHUNK), :]

    mine = ids[pl.ds(my_rows, CHUNK), :]
    hit = (mine >= 0) & (mine < LAT_DEV)
    my_bias = jnp.zeros((CHUNK, 128), F32)
    for h in range(8):
        row = jnp.broadcast_to(encb_v[:, 128 * h:128 * h + 128], (CHUNK, 128))
        my_bias = jnp.where(
            mine >> 7 == h, jnp.take_along_axis(row, mine & 127, 1, mode="promise_in_bounds"), my_bias)

    high = local >> 7
    inside = (local >= 0) & (local < LAT_DEV)
    field = (lax.broadcasted_iota(I32, local.shape, 0) + 1) << ((high & 3) * 8)
    lo_s[...] = local & 127
    w0_s[...] = jnp.where(inside & (high < 4), field, 0)
    w1_s[...] = jnp.where(inside & (high >= 4), field, 0)

    def fields(it, carry):
        cols = pl.ds(pl.multiple_of((it // 4) * 128, 128), 128)
        low = pl.multiple_of((it % 4) * 32, 32)
        iota = lax.broadcasted_iota(I32, (32, 128), 0) + low

        def eight(k8, acc):
            acc_0, acc_1 = acc
            rows = pl.ds(pl.multiple_of(k8 * 8, 8), 8)
            lo_8, w0_8, w1_8 = lo_s[rows, cols], w0_s[rows, cols], w1_s[rows, cols]
            for k in range(8):
                same = jnp.broadcast_to(lo_8[k:k + 1, :], (32, 128)) == iota
                acc_0 = acc_0 | jnp.where(same, jnp.broadcast_to(w0_8[k:k + 1, :], (32, 128)), 0)
                acc_1 = acc_1 | jnp.where(same, jnp.broadcast_to(w1_8[k:k + 1, :], (32, 128)), 0)
            return acc_0, acc_1

        zero = jnp.zeros((32, 128), I32)
        acc_0, acc_1 = lax.fori_loop(0, KMAX // 8, eight, (zero, zero))
        u0_t[pl.ds(low, 32), cols] = acc_0
        u1_t[pl.ds(low, 32), cols] = acc_1
        return carry

    lax.fori_loop(0, 16, fields, 0)
    u0[...] = u0_t[...].T
    u1[...] = u1_t[...].T

    loads[4].wait()
    latent = lax.broadcasted_iota(I32, (1, LAT_DEV), 1) + first
    for g in range(GROUPS):
        keep = jnp.where(latent < ends_ref[g], 1.0, 0.0).astype(BF16)
        masked_dec[MAIN * g:MAIN * g + MAIN, :] = dec_v[:MAIN, :] * keep
        at = GROUPS * MAIN + REM * g
        masked_dec[at:at + REM, :] = dec_v[MAIN:, :] * keep

    for j in range(len(PLANE)):
        a1_copy(j).wait_recv()
    total = jnp.zeros((CHUNK, 128), F32)
    for w in range(N_WID):
        total = total + a1_slot[w].astype(F32)
    acts_c[pl.ds(my_rows, CHUNK), :] = jnp.where(
        hit, jnp.maximum(total + my_bias, 0.0), 0.0).astype(BF16)

    def a2_copy(j):
        rows = acts_c.at[pl.ds(my_rows, CHUNK), :]
        return send(rows, rows, a2_send.at[j], a2_recv.at[j], in_plane(j))

    for j in range(len(PLANE)):
        a2_copy(j).start()
        pending.append(a2_copy(j))

    lane_16 = lax.broadcasted_iota(I32, (16, 128), 1)

    def densify(w):
        packed = acts_c[pl.ds(pl.multiple_of(w * CHUNK, CHUNK), CHUNK), :].astype(F32)
        for half in range(2):
            values = pltpu.roll(packed, 1 + KMAX * half, 1)
            values = jnp.where((lane_16 >= 1) & (lane_16 <= KMAX), values, 0.0)
            rows = pl.ds(pl.multiple_of(half * (ROWS // 2) + w * CHUNK, CHUNK), CHUNK)
            words = (u0[rows, :], u1[rows, :])
            for h in range(8):
                slot = (words[h // 4] >> (8 * (h % 4))) & 127
                dens[rows, 128 * h:128 * h + 128] = jnp.take_along_axis(
                    values, slot, 1, mode="promise_in_bounds").astype(BF16)

    densify(wid)
    for group in ARRIVALS:
        for j in group:
            a2_copy(j).wait_recv()
        for j in group:
            densify(plane(j, -1))

    def decode(half, cols):
        rows = pl.ds(pl.multiple_of(half * (ROWS // 2), ROWS // 2), ROWS // 2)
        return lax.dot_general(
            dens[rows, :], masked_dec[cols, :], (((1,), (1,)), ((), ())), preferred_element_type=F32
        ).astype(BF16)

    def sib_copy(i):
        cols = PIECES[i]
        return send(to_sib.at[:, cols], from_sib.at[:, cols], sib_send.at[i], sib_recv.at[i], sibling)

    def chip_sum(i, offset):
        p = lax.rem(z - offset + N_Z, N_Z)
        rows = pl.ds(pl.multiple_of(p * CHUNK, CHUNK), CHUNK)
        return own[rows, PIECES[i]].astype(F32) + from_sib[rows, PIECES[i]].astype(F32)

    def l1_copy(i, k):
        return send(l1_src.at[k, :, PIECES[i]], l1_slot.at[k, :, PIECES[i]], l1_send.at[i, k], l1_recv.at[i, k],
                    along_z(LEVEL_1[i % 2][k][1]))

    def l2_copy(i, j):
        step = -3 if CENTRES[j] > 0 else 3
        return send(l2_src.at[j, :, PIECES[i]], l2_slot.at[j, :, PIECES[i]], l2_send.at[i, j], l2_recv.at[i, j],
                    along_z(step))

    def l1_sum(i, centre):
        acc = chip_sum(i, centre)
        for k in members(i, centre):
            l1_copy(i, k).wait_recv()
            acc = acc + l1_slot[k, :, PIECES[i]].astype(F32)
        return acc

    for i, cols in enumerate(PIECES):
        to_sib[:, cols] = decode(1 - core, cols)
        sib_copy(i).start()
        pending.append(sib_copy(i))
    for i, cols in enumerate(PIECES):
        own[:, cols] = decode(core, cols)
        sib_copy(i).wait_recv()
        for k, (offset, _) in enumerate(LEVEL_1[i % 2]):
            l1_src[k, :, cols] = chip_sum(i, offset).astype(BF16)
            l1_copy(i, k).start()
            pending.append(l1_copy(i, k))

    for i, cols in enumerate(PIECES):
        for j in (0, 1):
            l2_src[j, :, cols] = l1_sum(i, CENTRES[j]).astype(BF16)
            l2_copy(i, j).start()
            pending.append(l2_copy(i, j))
    for i, cols in enumerate(PIECES):
        for j in (2, 3):
            acc = l1_sum(i, CENTRES[j])
            l2_copy(i, j - 2).wait_recv()
            l2_src[j, :, cols] = (acc + l2_slot[j - 2, :, cols].astype(F32)).astype(BF16)
            l2_copy(i, j).start()
            pending.append(l2_copy(i, j))
    parts = []
    for i, cols in enumerate(PIECES):
        acc = l1_sum(i, 0)
        for j in (2, 3):
            l2_copy(i, j).wait_recv()
            acc = acc + l2_slot[j, :, cols].astype(F32)
        parts.append(acc)
    prefix = jnp.concatenate(parts, axis=1)
    row_0 = core * (ROWS // 2) + z * CHUNK
    centered = xs[pl.ds(pl.multiple_of(row_0, CHUNK), CHUNK), :]
    err_tail = centered[:, MAIN:] - prefix[:, GROUPS * MAIN:]
    sq_tail = err_tail * err_tail
    row_16 = lax.broadcasted_iota(I32, (16, 128), 0)
    placed = jnp.zeros((16, 128), F32)
    for g in range(GROUPS):
        err = centered[:, :MAIN] - prefix[:, MAIN * g:MAIN * g + MAIN]
        sq = err * err
        sq = sq[:, :128] + sq[:, 128:] + jnp.where(lane_16 // REM == g, sq_tail, 0.0)
        loss = jnp.sum(sq, axis=1, keepdims=True)
        placed = placed + jnp.where(lane_16 == lax.rem(z + g, 8) * 16 + row_16, loss, 0.0)
    partial = jnp.sum(placed, axis=0, keepdims=True)

    def c1_copy(j):
        return send(c1_src, c1_slot.at[wid], c1_send.at[j], c1_recv.at[j], in_plane(j))

    c1_src[...] = partial
    for j in range(len(PLANE)):
        c1_copy(j).start()
        pending.append(c1_copy(j))
    c1_slot[wid] = partial
    for j in range(len(PLANE)):
        c1_copy(j).wait_recv()
    total_loss = c1_slot[0]
    for w in range(1, N_WID):
        total_loss = total_loss + c1_slot[w]
    total_loss = total_loss / (SHARD * N_WID)

    place = core * N_Z + z

    def c2_copy(j):
        dz, dc = COLUMN[j]
        target = (z + dz) % N_Z * 2 + (core + dc) % 2
        return send(c2_src, c2_slot.at[place], c2_send.at[j], c2_recv.at[j], (target, wid))

    c2_src[...] = total_loss
    for j in range(len(COLUMN)):
        c2_copy(j).start()
        pending.append(c2_copy(j))
    c2_slot[place] = total_loss
    for copy in pending:
        copy.wait_send()
    for j in range(len(COLUMN)):
        c2_copy(j).wait_recv()

    lane_8 = lax.broadcasted_iota(I32, (8, 128), 1)
    sub_8 = lax.broadcasted_iota(I32, (8, 128), 0)
    for b in range(ROWS // 128):
        block = jnp.concatenate([c2_slot[8 * b + m] for m in range(8)], axis=0)
        for g in range(GROUPS):
            line = jnp.sum(jnp.where(lane_8 // 16 == (sub_8 + g) % 8, block, 0.0), axis=0, keepdims=True)
            line = jnp.broadcast_to(line, (8, 128))
            if g:
                line = pltpu.roll(line, 128 - 16 * g, 1)
            out_ref[g:g + 1, 128 * b:128 * b + 128] = line[:1, :]


def body(model_acts, picks, group_ends, enc_weight, enc_bias, dec_weight, dec_bias):
    vmem, dma = pltpu.VMEM, pltpu.SemaphoreType.DMA
    half = ROWS // 2
    n_1, n_2, n_p = len(LEVEL_1[0]), len(CENTRES), len(PIECES)
    anywhere = pl.BlockSpec(memory_space=pl.ANY)
    losses = pl.pallas_call(
        kernel,
        out_shape=pltpu.VMEM((GROUPS, ROWS), F32),
        in_specs=[anywhere, anywhere, pl.BlockSpec(memory_space=pltpu.SMEM)] + [anywhere] * 3
        + [pl.BlockSpec(memory_space=pltpu.VMEM)],
        out_specs=pl.BlockSpec(memory_space=pltpu.VMEM),
        scratch_shapes=[
            vmem((SHARD, ROWS), BF16), vmem((KMAX, ROWS), I32), vmem((SHARD, LAT_DEV), BF16),
            vmem((1, LAT_DEV), F32), vmem((SHARD, LAT_DEV), BF16),
            vmem((ROWS, MAIN + 128), F32), vmem((ROWS, LAT_DEV), F32), vmem((half, 128), I32),
            vmem((KMAX, ROWS), I32), vmem((KMAX, ROWS), I32), vmem((KMAX, ROWS), I32),
            vmem((128, ROWS), I32), vmem((128, ROWS), I32), vmem((ROWS, 128), I32), vmem((ROWS, 128), I32),
            vmem((WIDE, LAT_DEV), BF16),
            vmem((half, 128), BF16), vmem((N_WID, CHUNK, 128), BF16), vmem((half, 128), BF16),
            vmem((ROWS, LAT_DEV), BF16), vmem((half, WIDE), BF16), vmem((half, WIDE), BF16),
            vmem((half, WIDE), BF16),
            vmem((n_1, CHUNK, WIDE), BF16), vmem((n_1, CHUNK, WIDE), BF16),
            vmem((n_2, CHUNK, WIDE), BF16), vmem((n_2, CHUNK, WIDE), BF16),
            vmem((1, 128), F32), vmem((N_WID, 1, 128), F32), vmem((1, 128), F32), vmem((N_LAT, 1, 128), F32),
            dma((5,)), dma((N_WID,)), dma((N_WID,)), dma((N_WID,)), dma((N_WID,)), dma((n_p,)), dma((n_p,)),
            dma((n_p, n_1)), dma((n_p, n_1)), dma((n_p, n_2)), dma((n_p, n_2)),
            dma((N_WID,)), dma((N_WID,)), dma((N_LAT,)), dma((N_LAT,)),
        ],
        compiler_params=pltpu.CompilerParams(
            collective_id=0, has_side_effects=True, vmem_limit_bytes=56 * 2 ** 20),
    )(
        model_acts.T, picks.T, group_ends, enc_weight, enc_bias.reshape(1, -1), dec_weight.T,
        dec_bias,
    )
    return losses.T


def solution(mesh):
    placed = (P(None, "wid"), P(), P(), P("wid", "lat"), P("lat"), P("lat", "wid"), P("wid"))
    return jax.shard_map(body, mesh=mesh, in_specs=placed, out_specs=P(), check_vma=False)
```

```python
import jax
import jax.numpy as jnp
from jax import lax
from jax.experimental import pallas as pl
from jax.experimental.pallas import tpu as pltpu
from jax.sharding import PartitionSpec as P

F32, BF16, I32 = jnp.float32, jnp.bfloat16, jnp.int32
ROWS, KMAX, GROUPS = 512, 64, 4
SHARD, MAIN = 288, 256
REM = SHARD - MAIN
LAT_DEV = 1024
EXTRACT = 64
N_LAT, N_WID, N_Z = 32, 16, 16
CHUNK = 16
WIDE = GROUPS * SHARD

LEVEL_1 = (
    (5, 1), (7, -1), (-7, 1), (-5, -1), (8, -2),
    (2, 1), (4, -1), (-4, 1), (-2, -1),
    (1, -1), (-1, 1),
)
LEVEL_1 = (LEVEL_1, LEVEL_1[:4] + ((-8, 2),) + LEVEL_1[5:])
CENTRES = (6, -6, 3, -3)
PIECES = (slice(0, 256), slice(256, WIDE))
Z_PEERS = (3, -3, 2, -2, 1, -1)


def ring(step, size):
    return min(step % size, -step % size)


PLANE = sorted(
    ((dx, dy) for dx in range(4) for dy in range(4) if dx or dy),
    key=lambda d: -(ring(d[0], 4) + ring(d[1], 4)))
COLUMN = sorted(
    ((dz, dc) for dz in range(N_Z) for dc in range(2) if dz or dc), key=lambda d: -ring(d[0], N_Z))
ARRIVALS = (range(14, 10, -1), range(10, 4, -1), range(4, -1, -1))


def members(i, centre):
    return [k for k, (offset, dz) in enumerate(LEVEL_1[i % 2]) if offset + dz == centre]


def kernel(
    x_hbm, picks_hbm, ends_ref, encw_hbm, encb_hbm, dec_hbm, decb_v, out_ref,
    x_v, picks_v, encw_v, encb_v, dec_v,
    xs, part, ids, lo_s, w0_s, w1_s, u0_t, u1_t, u0, u1, masked_dec,
    a1_src, a1_slot, acts_c, dens, to_sib, own, from_sib,
    l1_src, l1_slot, l2_src, l2_slot, c1_src, c1_slot, c2_src, c2_slot,
    in_sem, a1_send, a1_recv, a2_send, a2_recv, sib_send, sib_recv,
    l1_send, l1_recv, l2_send, l2_recv, c1_send, c1_recv, c2_send, c2_recv,
):
    lat = lax.axis_index("lat")
    wid = lax.axis_index("wid")
    z, core = lat // 2, lat % 2
    first = lat * LAT_DEV

    def plane(j, sign=1):
        dx, dy = PLANE[j]
        return (wid // 4 + 4 + sign * dx) % 4 * 4 + (wid % 4 + 4 + sign * dy) % 4

    def in_plane(j):
        return (lat, plane(j))

    def along_z(step):
        return (lax.rem(z + step + N_Z, N_Z) * 2 + core, wid)

    sibling = (lat + 1 - 2 * core, wid)

    def send(src, dst, s_sem, r_sem, device):
        return pltpu.make_async_remote_copy(
            src_ref=src, dst_ref=dst, send_sem=s_sem, recv_sem=r_sem,
            device_id=device, device_id_type=pl.DeviceIdType.MESH,
        )

    loads = [
        pltpu.make_async_copy(src, dst, in_sem.at[i])
        for i, (src, dst) in enumerate(
            ((x_hbm, x_v), (encw_hbm, encw_v), (picks_hbm, picks_v),
             (encb_hbm, encb_v), (dec_hbm, dec_v))
        )
    ]
    for load in loads:
        load.start()
    barrier = pltpu.get_barrier_semaphore()

    def greet(device):
        pl.semaphore_signal(barrier, inc=1, device_id=device, device_id_type=pl.DeviceIdType.MESH)

    for step in Z_PEERS:
        greet(along_z(step))
    for j in range(len(PLANE)):
        greet(in_plane(j))
    greet(sibling)
    pending = []

    for load in loads[:4]:
        load.wait()
    x_t = x_v[...].astype(F32)
    tail = x_t[MAIN:, :]
    lanes_1 = lax.broadcasted_iota(I32, (1, 128), 1)
    bias_tail = jnp.concatenate([decb_v[MAIN:].reshape(1, REM), jnp.zeros((1, 128 - REM), F32)], axis=1)
    bias_tail = jnp.where(lanes_1 < REM, bias_tail, 0.0)
    bias_tail = jnp.broadcast_to(bias_tail, (8, 128))
    bias_tail = (bias_tail + pltpu.roll(bias_tail, REM, 1)) + (
        pltpu.roll(bias_tail, 2 * REM, 1) + pltpu.roll(bias_tail, 3 * REM, 1))
    bias = jnp.concatenate([decb_v[:MAIN].reshape(1, MAIN), bias_tail[:1, :]], axis=1)
    xs[...] = jnp.concatenate([x_t, tail, tail, tail], axis=0).T - bias
    part[...] = jnp.dot(
        xs[:, :SHARD].astype(BF16), encw_v[...], preferred_element_type=F32
    )

    local = picks_v[...] - first
    ids[...] = jnp.concatenate([local[:, :ROWS // 2], local[:, ROWS // 2:]], axis=0).T

    lane_e = lax.broadcasted_iota(I32, (EXTRACT, 128), 1)

    def extract(i, carry):
        r = pl.multiple_of(i * EXTRACT, EXTRACT)
        r_2 = pl.multiple_of(i * EXTRACT + ROWS // 2, EXTRACT)
        where = ids[pl.ds(r, EXTRACT), :]
        lo, hi = where & 127, where >> 7
        got = jnp.zeros((EXTRACT, 128), F32)
        for h in range(8):
            cols = slice(128 * h, 128 * h + 128)
            here = jnp.where(
                lane_e < KMAX,
                jnp.take_along_axis(part[pl.ds(r, EXTRACT), cols], lo, 1, mode="promise_in_bounds"),
                jnp.take_along_axis(part[pl.ds(r_2, EXTRACT), cols], lo, 1, mode="promise_in_bounds"),
            )
            got = jnp.where(hi == h, here, got)
        a1_src[pl.ds(r, EXTRACT), :] = got.astype(BF16)
        return carry

    lax.fori_loop(0, ROWS // 2 // EXTRACT, extract, 0)

    pl.semaphore_wait(barrier, len(Z_PEERS) + N_WID)
    def a1_copy(j):
        target = plane(j)
        rows = pl.ds(pl.multiple_of(target * CHUNK, CHUNK), CHUNK)
        return send(a1_src.at[rows], a1_slot.at[wid], a1_send.at[j], a1_recv.at[j], (lat, target))

    for j in range(len(PLANE)):
        a1_copy(j).start()
        pending.append(a1_copy(j))
    my_rows = pl.multiple_of(wid * CHUNK, CHUNK)
    a1_slot[wid] = a1_src[pl.ds(my_rows, CHUNK), :]

    mine = ids[pl.ds(my_rows, CHUNK), :]
    hit = (mine >= 0) & (mine < LAT_DEV)
    my_bias = jnp.zeros((CHUNK, 128), F32)
    for h in range(8):
        row = jnp.broadcast_to(encb_v[:, 128 * h:128 * h + 128], (CHUNK, 128))
        my_bias = jnp.where(
            mine >> 7 == h, jnp.take_along_axis(row, mine & 127, 1, mode="promise_in_bounds"), my_bias)

    high = local >> 7
    inside = (local >= 0) & (local < LAT_DEV)
    field = (lax.broadcasted_iota(I32, local.shape, 0) + 1) << ((high & 3) * 8)
    lo_s[...] = local & 127
    w0_s[...] = jnp.where(inside & (high < 4), field, 0)
    w1_s[...] = jnp.where(inside & (high >= 4), field, 0)

    def fields(it, carry):
        cols = pl.ds(pl.multiple_of((it // 4) * 128, 128), 128)
        low = pl.multiple_of((it % 4) * 32, 32)
        iota = lax.broadcasted_iota(I32, (32, 128), 0) + low

        def eight(k8, acc):
            acc_0, acc_1 = acc
            rows = pl.ds(pl.multiple_of(k8 * 8, 8), 8)
            lo_8, w0_8, w1_8 = lo_s[rows, cols], w0_s[rows, cols], w1_s[rows, cols]
            for k in range(8):
                same = jnp.broadcast_to(lo_8[k:k + 1, :], (32, 128)) == iota
                acc_0 = acc_0 | jnp.where(same, jnp.broadcast_to(w0_8[k:k + 1, :], (32, 128)), 0)
                acc_1 = acc_1 | jnp.where(same, jnp.broadcast_to(w1_8[k:k + 1, :], (32, 128)), 0)
            return acc_0, acc_1

        zero = jnp.zeros((32, 128), I32)
        acc_0, acc_1 = lax.fori_loop(0, KMAX // 8, eight, (zero, zero))
        u0_t[pl.ds(low, 32), cols] = acc_0
        u1_t[pl.ds(low, 32), cols] = acc_1
        return carry

    lax.fori_loop(0, 16, fields, 0)
    u0[...] = u0_t[...].T
    u1[...] = u1_t[...].T

    loads[4].wait()
    latent = lax.broadcasted_iota(I32, (1, LAT_DEV), 1) + first
    for g in range(GROUPS):
        keep = jnp.where(latent < ends_ref[g], 1.0, 0.0).astype(BF16)
        masked_dec[MAIN * g:MAIN * g + MAIN, :] = dec_v[:MAIN, :] * keep
        at = GROUPS * MAIN + REM * g
        masked_dec[at:at + REM, :] = dec_v[MAIN:, :] * keep

    for j in range(len(PLANE)):
        a1_copy(j).wait_recv()
    total = jnp.zeros((CHUNK, 128), F32)
    for w in range(N_WID):
        total = total + a1_slot[w].astype(F32)
    acts_c[pl.ds(my_rows, CHUNK), :] = jnp.where(
        hit, jnp.maximum(total + my_bias, 0.0), 0.0).astype(BF16)

    def a2_copy(j):
        rows = acts_c.at[pl.ds(my_rows, CHUNK), :]
        return send(rows, rows, a2_send.at[j], a2_recv.at[j], in_plane(j))

    for j in range(len(PLANE)):
        a2_copy(j).start()
        pending.append(a2_copy(j))

    lane_16 = lax.broadcasted_iota(I32, (16, 128), 1)

    def densify(w):
        packed = acts_c[pl.ds(pl.multiple_of(w * CHUNK, CHUNK), CHUNK), :].astype(F32)
        for half in range(2):
            values = pltpu.roll(packed, 1 + KMAX * half, 1)
            values = jnp.where((lane_16 >= 1) & (lane_16 <= KMAX), values, 0.0)
            rows = pl.ds(pl.multiple_of(half * (ROWS // 2) + w * CHUNK, CHUNK), CHUNK)
            words = (u0[rows, :], u1[rows, :])
            for h in range(8):
                slot = (words[h // 4] >> (8 * (h % 4))) & 127
                dens[rows, 128 * h:128 * h + 128] = jnp.take_along_axis(
                    values, slot, 1, mode="promise_in_bounds").astype(BF16)

    densify(wid)
    for group in ARRIVALS:
        for j in group:
            a2_copy(j).wait_recv()
        for j in group:
            densify(plane(j, -1))

    def decode(half, cols):
        rows = pl.ds(pl.multiple_of(half * (ROWS // 2), ROWS // 2), ROWS // 2)
        return lax.dot_general(
            dens[rows, :], masked_dec[cols, :], (((1,), (1,)), ((), ())), preferred_element_type=F32
        ).astype(BF16)

    def sib_copy(i):
        cols = PIECES[i]
        return send(to_sib.at[:, cols], from_sib.at[:, cols], sib_send.at[i], sib_recv.at[i], sibling)

    def chip_sum(i, offset):
        p = lax.rem(z - offset + N_Z, N_Z)
        rows = pl.ds(pl.multiple_of(p * CHUNK, CHUNK), CHUNK)
        return own[rows, PIECES[i]].astype(F32) + from_sib[rows, PIECES[i]].astype(F32)

    def l1_copy(i, k):
        return send(l1_src.at[k, :, PIECES[i]], l1_slot.at[k, :, PIECES[i]], l1_send.at[i, k], l1_recv.at[i, k],
                    along_z(LEVEL_1[i % 2][k][1]))

    def l2_copy(i, j):
        step = -3 if CENTRES[j] > 0 else 3
        return send(l2_src.at[j, :, PIECES[i]], l2_slot.at[j, :, PIECES[i]], l2_send.at[i, j], l2_recv.at[i, j],
                    along_z(step))

    def l1_sum(i, centre):
        acc = chip_sum(i, centre)
        for k in members(i, centre):
            l1_copy(i, k).wait_recv()
            acc = acc + l1_slot[k, :, PIECES[i]].astype(F32)
        return acc

    for i, cols in enumerate(PIECES):
        to_sib[:, cols] = decode(1 - core, cols)
        sib_copy(i).start()
        pending.append(sib_copy(i))
    for i, cols in enumerate(PIECES):
        own[:, cols] = decode(core, cols)
        sib_copy(i).wait_recv()
        for k, (offset, _) in enumerate(LEVEL_1[i % 2]):
            l1_src[k, :, cols] = chip_sum(i, offset).astype(BF16)
            l1_copy(i, k).start()
            pending.append(l1_copy(i, k))

    for i, cols in enumerate(PIECES):
        for j in (0, 1):
            l2_src[j, :, cols] = l1_sum(i, CENTRES[j]).astype(BF16)
            l2_copy(i, j).start()
            pending.append(l2_copy(i, j))
    for i, cols in enumerate(PIECES):
        for j in (2, 3):
            acc = l1_sum(i, CENTRES[j])
            l2_copy(i, j - 2).wait_recv()
            l2_src[j, :, cols] = (acc + l2_slot[j - 2, :, cols].astype(F32)).astype(BF16)
            l2_copy(i, j).start()
            pending.append(l2_copy(i, j))
    parts = []
    for i, cols in enumerate(PIECES):
        acc = l1_sum(i, 0)
        for j in (2, 3):
            l2_copy(i, j).wait_recv()
            acc = acc + l2_slot[j, :, cols].astype(F32)
        parts.append(acc)
    prefix = jnp.concatenate(parts, axis=1)
    row_0 = core * (ROWS // 2) + z * CHUNK
    centered = xs[pl.ds(pl.multiple_of(row_0, CHUNK), CHUNK), :]
    err_tail = centered[:, MAIN:] - prefix[:, GROUPS * MAIN:]
    sq_tail = err_tail * err_tail
    row_16 = lax.broadcasted_iota(I32, (16, 128), 0)
    placed = jnp.zeros((16, 128), F32)
    for g in range(GROUPS):
        err = centered[:, :MAIN] - prefix[:, MAIN * g:MAIN * g + MAIN]
        sq = err * err
        sq = sq[:, :128] + sq[:, 128:] + jnp.where(lane_16 // REM == g, sq_tail, 0.0)
        loss = jnp.sum(sq, axis=1, keepdims=True)
        placed = placed + jnp.where(lane_16 == lax.rem(z + g, 8) * 16 + row_16, loss, 0.0)
    partial = jnp.sum(placed, axis=0, keepdims=True)

    def c1_copy(j):
        return send(c1_src, c1_slot.at[wid], c1_send.at[j], c1_recv.at[j], in_plane(j))

    c1_src[...] = partial
    for j in range(len(PLANE)):
        c1_copy(j).start()
        pending.append(c1_copy(j))
    c1_slot[wid] = partial
    for j in range(len(PLANE)):
        c1_copy(j).wait_recv()
    total_loss = c1_slot[0]
    for w in range(1, N_WID):
        total_loss = total_loss + c1_slot[w]
    total_loss = total_loss / (SHARD * N_WID)

    place = core * N_Z + z

    def c2_copy(j):
        dz, dc = COLUMN[j]
        target = (z + dz) % N_Z * 2 + (core + dc) % 2
        return send(c2_src, c2_slot.at[place], c2_send.at[j], c2_recv.at[j], (target, wid))

    c2_src[...] = total_loss
    for j in range(len(COLUMN)):
        c2_copy(j).start()
        pending.append(c2_copy(j))
    c2_slot[place] = total_loss
    for copy in pending:
        copy.wait_send()
    for j in range(len(COLUMN)):
        c2_copy(j).wait_recv()

    lane_8 = lax.broadcasted_iota(I32, (8, 128), 1)
    sub_8 = lax.broadcasted_iota(I32, (8, 128), 0)
    for b in range(ROWS // 128):
        block = jnp.concatenate([c2_slot[8 * b + m] for m in range(8)], axis=0)
        for g in range(GROUPS):
            line = jnp.sum(jnp.where(lane_8 // 16 == (sub_8 + g) % 8, block, 0.0), axis=0, keepdims=True)
            line = jnp.broadcast_to(line, (8, 128))
            if g:
                line = pltpu.roll(line, 128 - 16 * g, 1)
            out_ref[g:g + 1, 128 * b:128 * b + 128] = line[:1, :]


def body(model_acts, picks, group_ends, enc_weight, enc_bias, dec_weight, dec_bias):
    vmem, dma = pltpu.VMEM, pltpu.SemaphoreType.DMA
    half = ROWS // 2
    n_1, n_2, n_p = len(LEVEL_1[0]), len(CENTRES), len(PIECES)
    anywhere = pl.BlockSpec(memory_space=pl.ANY)
    losses = pl.pallas_call(
        kernel,
        out_shape=pltpu.VMEM((GROUPS, ROWS), F32),
        in_specs=[anywhere, anywhere, pl.BlockSpec(memory_space=pltpu.SMEM)] + [anywhere] * 3
        + [pl.BlockSpec(memory_space=pltpu.VMEM)],
        out_specs=pl.BlockSpec(memory_space=pltpu.VMEM),
        scratch_shapes=[
            vmem((SHARD, ROWS), BF16), vmem((KMAX, ROWS), I32), vmem((SHARD, LAT_DEV), BF16),
            vmem((1, LAT_DEV), F32), vmem((SHARD, LAT_DEV), BF16),
            vmem((ROWS, MAIN + 128), F32), vmem((ROWS, LAT_DEV), F32), vmem((half, 128), I32),
            vmem((KMAX, ROWS), I32), vmem((KMAX, ROWS), I32), vmem((KMAX, ROWS), I32),
            vmem((128, ROWS), I32), vmem((128, ROWS), I32), vmem((ROWS, 128), I32), vmem((ROWS, 128), I32),
            vmem((WIDE, LAT_DEV), BF16),
            vmem((half, 128), BF16), vmem((N_WID, CHUNK, 128), BF16), vmem((half, 128), BF16),
            vmem((ROWS, LAT_DEV), BF16), vmem((half, WIDE), BF16), vmem((half, WIDE), BF16),
            vmem((half, WIDE), BF16),
            vmem((n_1, CHUNK, WIDE), BF16), vmem((n_1, CHUNK, WIDE), BF16),
            vmem((n_2, CHUNK, WIDE), BF16), vmem((n_2, CHUNK, WIDE), BF16),
            vmem((1, 128), F32), vmem((N_WID, 1, 128), F32), vmem((1, 128), F32), vmem((N_LAT, 1, 128), F32),
            dma((5,)), dma((N_WID,)), dma((N_WID,)), dma((N_WID,)), dma((N_WID,)), dma((n_p,)), dma((n_p,)),
            dma((n_p, n_1)), dma((n_p, n_1)), dma((n_p, n_2)), dma((n_p, n_2)),
            dma((N_WID,)), dma((N_WID,)), dma((N_LAT,)), dma((N_LAT,)),
        ],
        compiler_params=pltpu.CompilerParams(
            collective_id=0, has_side_effects=True, vmem_limit_bytes=56 * 2 ** 20),
    )(
        model_acts.T, picks.T, group_ends, enc_weight, enc_bias.reshape(1, -1), dec_weight.T,
        dec_bias,
    )
    return losses.T


def solution(mesh):
    placed = (P(None, "wid"), P(), P(), P("wid", "lat"), P("lat"), P("lat", "wid"), P("wid"))
    return jax.shard_map(body, mesh=mesh, in_specs=placed, out_specs=P(), check_vma=False)
```
